256 devices in a mesh: dp: 8 (over z_hi, y), expert: 32 (over z_lo, x, core).
Axes of the slice: x: 4, y: 4, z: 8 (z_hi: 2, z_lo: 4; z = z_hi * 4 + z_lo), core: 2. Of those that a mesh axis runs over, the one named last changes fastest.
Arguments:
- tokens: bfloat16 [32768, 2048], P(('dp', 'expert')), may hold values from -6 to 6
- cotangent: bfloat16 [32768, 2048], P(('dp', 'expert')), may hold values from -6 to 6
- gate_probs: float32 [32768, 2], P(('dp', 'expert')), may hold values from 0.2 to 1
- expert_ids: int32 [32768, 2], P(('dp', 'expert')), may hold values from 0 to 31, as said below
- route_slots: int32 [32768, 2], P(('dp', 'expert')), may hold values from 0 to 4, as said below
- hot_mask: int32 [32], replicated, may hold values from 0 to 1, as said below
- w_up: bfloat16 [32, 2048, 4096], P('expert', None, 'dp'), may hold values from -0.125 to 0.125
- w_down: bfloat16 [32, 4096, 2048], P('expert', 'dp'), may hold values from -0.09375 to 0.09375
Outputs:
- layer_out: bfloat16 [32768, 2048], P(('dp', 'expert'))
- grad_tokens: bfloat16 [32768, 2048], P(('dp', 'expert'))
- grad_up: bfloat16 [32, 2048, 4096], P(None, 'expert', 'dp')
- grad_down: bfloat16 [32, 2048, 4096], P(None, 'expert', 'dp')
The draws below stay inside these ranges and needn't reach their ends.
Inputs may be any that keep to these rules, and one draw needn't show every extreme that they name: `expert_ids`: A token's two experts differ. Only first choices name the hot expert. Every device's 128 tokens (aligned blocks) name the hot expert at least 4 + 1 times. route_slots[t, c] is the rank of route (t, c) among the routes of the same device's 128 tokens (aligned blocks) to the same expert, counting all first choices in token order before all second choices, capped at 4. `hot_mask`: exactly one entry is 1.
All inputs are finite; a program needn't handle non-finite values.
Results may differ from the reference program's by a relative error of at most 0.014.
Values may be sent and summed in bfloat16 or wider, within the bound.
A program may use at most 128 MiB of HBM per device.

```python
import jax
import jax.numpy as jnp
from jax import lax

D = 2048
FF = 4096
TOK_DEV = 128
CAP = 2
HCAP = 4
EXPERTS = 32
TOKENS = 32768
N_DP = 8
N_EXPERT = 32


def route_plan(key):
    base = jax.random.fold_in(key, 11)
    key_hot, key_busy, key_order, key_first, key_second = jax.random.split(base, 5)
    blocks = N_DP * N_EXPERT
    hot_expert = jax.random.randint(key_hot, (), 0, EXPERTS)
    busy = (hot_expert + jax.random.randint(key_busy, (N_DP,), 1, EXPERTS)) % EXPERTS
    busy_block = jnp.repeat(busy, N_EXPERT)
    block_keys = jax.random.split(key_order, blocks)
    position_rank = jax.vmap(lambda one_key: jax.random.permutation(one_key, TOK_DEV))(block_keys)
    first_free = jax.random.randint(key_first, (blocks, TOK_DEV), 0, EXPERTS)
    first_pick = jnp.where(position_rank <= CAP, busy_block[:, None], jnp.where(position_rank <= CAP + HCAP + 1, hot_expert, first_free))
    offsets = jax.random.randint(key_second, (blocks, TOK_DEV), 1, EXPERTS - 1)
    second_pick = (hot_expert + offsets) % EXPERTS
    second_pick = jnp.where(second_pick == first_pick, (hot_expert + EXPERTS - 1) % EXPERTS, second_pick)
    expert_table = jnp.stack([first_pick, second_pick], axis=-1).reshape(TOKENS, 2)
    ordered = jnp.concatenate([first_pick, second_pick], axis=1)
    onehot = (ordered[:, :, None] == jnp.arange(EXPERTS)[None, None, :]).astype(jnp.int32)
    earlier = jnp.cumsum(onehot, axis=1) - onehot
    ranks = jnp.minimum(jnp.sum(earlier * onehot, axis=2), HCAP)
    slot_table = jnp.stack([ranks[:, :TOK_DEV], ranks[:, TOK_DEV:]], axis=-1).reshape(TOKENS, 2)
    mask_table = (jnp.arange(EXPERTS) == hot_expert).astype(jnp.int32)
    return (expert_table.astype(jnp.int32), slot_table.astype(jnp.int32), mask_table)


def draw_expert_ids(key, part):
    return route_plan(key)[0]


def draw_route_slots(key, part):
    return route_plan(key)[1]


def draw_hot_mask(key, part):
    return route_plan(key)[2]


def block_scale(stream_key, shape, shards, least, top_value):
    factor_of = 1.0
    for dim, blocks in shards:
        steps = jax.random.uniform(jax.random.fold_in(jax.random.fold_in(stream_key, 6), dim), (blocks,), jnp.float32, least / len(shards), top_value / len(shards))
        factor_of = factor_of * jnp.repeat(jnp.exp(steps), shape[dim] // blocks).reshape((-1,) + (1,) * (len(shape) - 1 - dim))
    return factor_of


def gaussian(own_key, dims, width, bound, pieces=(), held_as=jnp.bfloat16):
    drawn = width * jax.random.normal(own_key, dims, jnp.float32)
    if pieces:
        drawn = drawn * block_scale(own_key, dims, pieces, -0.22, 0.18)
    return jnp.clip(drawn, -bound, bound).astype(held_as)


def setup_inputs(seed: int = 0) -> dict:
    keys = jax.random.split(jax.random.key(seed), 9)
    tokens = gaussian(keys[0], (TOKENS, D), 1.0, 6.0, ((0, 256),))
    cotangent = gaussian(keys[1], (TOKENS, D), 1.0, 6.0, ((0, 256),))
    gate_probs = jnp.clip(0.2 + 0.8 * jax.random.uniform(keys[2], (TOKENS, 2), jnp.float32) ** block_scale(keys[2], (TOKENS, 2), ((0, 256),), -0.2, 0.2), 0.2, 1.0)
    expert_ids = draw_expert_ids(jax.random.fold_in(keys[8], 71), 0)
    route_slots = draw_route_slots(jax.random.fold_in(keys[8], 71), 0)
    hot_mask = draw_hot_mask(jax.random.fold_in(keys[8], 71), 0)
    w_up = gaussian(keys[6], (EXPERTS, D, FF), D ** -0.5, 0.125, ((0, 32), (2, 8)))
    w_down = gaussian(keys[7], (EXPERTS, FF, D), FF ** -0.5, 0.09375, ((0, 32), (1, 8)))
    return {"tokens": tokens, "cotangent": cotangent, "gate_probs": gate_probs, "expert_ids": expert_ids, "route_slots": route_slots, "hot_mask": hot_mask, "w_up": w_up, "w_down": w_down}


def gelu_pair(preact):
    normal_cdf = 0.5 * (1.0 + lax.erf(preact * 0.7071067811865476))
    density = jnp.exp(-0.5 * preact * preact) * 0.3989422804014327
    return preact * normal_cdf, normal_cdf + preact * density


def reference(tokens, cotangent, gate_probs, expert_ids, route_slots, hot_mask, w_up, w_down):
    blocks = N_DP * N_EXPERT
    route_count = TOKENS * 2
    slice_width = FF // N_DP
    route_index = jnp.arange(route_count, dtype=jnp.int32)
    flat_expert = expert_ids.reshape(-1).astype(jnp.int32)
    flat_slot = route_slots.reshape(-1).astype(jnp.int32)
    flat_block = ((route_index // 2) // TOK_DEV).astype(jnp.int32)
    is_hot = jnp.take(hot_mask, flat_expert) > 0
    capacity = jnp.where(is_hot, HCAP, CAP).astype(jnp.int32)
    kept_route = flat_slot < capacity
    target = jnp.where(kept_route, flat_slot, HCAP).astype(jnp.int32)
    route_table = jnp.full((EXPERTS, blocks, HCAP), -1, dtype=jnp.int32)
    route_table = route_table.at[flat_expert, flat_block, target].set(route_index, mode="drop")
    routed = (gate_probs[:, :, None] * cotangent[:, None, :].astype(jnp.float32)).astype(jnp.bfloat16)
    routed = routed.reshape(route_count, D)
    tokens_rep = jnp.repeat(tokens, 2, axis=0)

    def expert_step(totals, inputs):
        table_rows, up_weight, down_weight = inputs
        rows_index = table_rows.reshape(-1).astype(jnp.int32)
        filled = rows_index >= 0
        safe_index = jnp.maximum(rows_index, 0).astype(jnp.int32)
        rows_x = jnp.where(filled[:, None], tokens_rep[safe_index], jnp.zeros((), jnp.bfloat16))
        rows_g = jnp.where(filled[:, None], routed[safe_index], jnp.zeros((), jnp.bfloat16))
        row_count = rows_x.shape[0]
        preact = jnp.dot(rows_x, up_weight, preferred_element_type=jnp.float32)
        gelu_value, gelu_slope = gelu_pair(preact)
        activation = gelu_value.astype(jnp.bfloat16)
        partials = jnp.einsum("rjf,jfd->jrd",
                              activation.reshape(row_count, N_DP, slice_width).astype(jnp.float32),
                              down_weight.reshape(N_DP, slice_width, D).astype(jnp.float32))
        rounded = lax.optimization_barrier(partials.astype(jnp.bfloat16))
        expert_out = jnp.sum(rounded.astype(jnp.float32), axis=0).astype(jnp.bfloat16)
        d_act = jnp.dot(rows_g, down_weight.T, preferred_element_type=jnp.float32)
        d_pre = (d_act * gelu_slope).astype(jnp.bfloat16)
        back_partials = jnp.einsum("rjf,djf->jrd",
                                   d_pre.reshape(row_count, N_DP, slice_width).astype(jnp.float32),
                                   up_weight.reshape(D, N_DP, slice_width).astype(jnp.float32))
        back_rounded = lax.optimization_barrier(back_partials.astype(jnp.bfloat16))
        route_back = jnp.sum(back_rounded.astype(jnp.float32), axis=0).astype(jnp.bfloat16)
        grad_in = jnp.dot(rows_x.T, d_pre, preferred_element_type=jnp.float32).astype(jnp.bfloat16)
        grad_out = jnp.dot(rows_g.T, activation, preferred_element_type=jnp.float32).astype(jnp.bfloat16)
        out_total = totals[0].at[safe_index].add(jnp.where(filled[:, None], expert_out.astype(jnp.float32), jnp.zeros((), jnp.float32)))
        back_total = totals[1].at[safe_index].add(jnp.where(filled[:, None], route_back.astype(jnp.float32), jnp.zeros((), jnp.float32)))
        return (out_total, back_total), (grad_in, grad_out)

    zero_routes = jnp.zeros((route_count, D), jnp.float32)
    totals, grads = lax.scan(expert_step, (zero_routes, zero_routes), (route_table, w_up, w_down))
    out_total, back_total = totals
    grad_up, grad_down = grads
    layer_out = jnp.sum(gate_probs[:, :, None] * out_total.reshape(TOKENS, 2, D), axis=1).astype(jnp.bfloat16)
    grad_tokens = jnp.sum(back_total.reshape(TOKENS, 2, D), axis=1).astype(jnp.bfloat16)
    return (layer_out, grad_tokens, grad_up, grad_down)
```

```python
import functools

import jax
import jax.numpy as jnp
from jax import lax
from jax.experimental import pallas as pl
from jax.experimental.pallas import tpu as pltpu
from jax.sharding import PartitionSpec as P

CAP = 2
HCAP = 4
MESH = pl.DeviceIdType.MESH
BF = jnp.bfloat16
F32 = jnp.float32
ANY = pl.BlockSpec(memory_space=pl.ANY)
VM = pl.BlockSpec(memory_space=pltpu.VMEM)
SM = pl.BlockSpec(memory_space=pltpu.SMEM)
DMA = pltpu.SemaphoreType.DMA
Z_OFFSETS = (0, 1, 7, 2, 6, 3, 5, 4)
LIMIT = 60 * 1024 * 1024


def sds(shape, dtype=BF):
    return jax.ShapeDtypeStruct(shape, dtype)


def iota(shape, dim):
    return lax.broadcasted_iota(jnp.int32, shape, dim)


def dot(a, b):
    return jnp.dot(a, b, preferred_element_type=F32)


def dot_nt(a, b):
    return lax.dot_general(a, b, (((1,), (1,)), ((), ())), preferred_element_type=F32)


def dot_tn(a, b):
    return lax.dot_general(a, b, (((0,), (0,)), ((), ())), preferred_element_type=F32)


def ones_where(cond):
    return jnp.where(cond, 1.0, 0.0).astype(BF)


def pack_kernel(hot_ref, tokens_ref, cot_ref, gate_ref, ids_ref, slots_ref, disp_ref, hrow_ref):
    hot = hot_ref[0]
    rows = disp_ref.shape[0]
    r = iota((rows, 128), 0)
    code = (r // 16) * CAP + (r // 4) % 2
    is_grad = (r // 8) % 2
    quarter = r % 4
    hr = iota((32, 128), 0)
    hcode = (hr // 4) % 4
    h_is_grad = hr // 16
    hquarter = hr % 4
    sel, hsel = [], []
    for c in range(2):
        ids = ids_ref[c : c + 1, :]
        slot = slots_ref[c : c + 1, :]
        is_hot = ids == hot
        place = jnp.where(jnp.logical_and(jnp.logical_not(is_hot), slot < CAP), ids * CAP + slot, -1)
        hplace = jnp.where(jnp.logical_and(is_hot, slot < HCAP), slot, -1)
        sel.append(code == place)
        hsel.append(hcode == hplace)
    cot = cot_ref[...].astype(F32)
    routed = [(gate_ref[:, c : c + 1] * cot).astype(BF) for c in range(2)]
    either = jnp.logical_or(sel[0], sel[1])
    heither = jnp.logical_or(hsel[0], hsel[1])
    out = jnp.zeros((rows, 512), F32)
    hout = jnp.zeros((32, 512), F32)
    for q in range(4):
        cols = slice(q * 512, (q + 1) * 512)
        at_q = quarter == q
        hat_q = hquarter == q
        parts = (
            (tokens_ref[:, cols], either, heither, 0),
            (routed[0][:, cols], sel[0], hsel[0], 1),
            (routed[1][:, cols], sel[1], hsel[1], 1),
        )
        for data, s, hs, kind in parts:
            m = ones_where(jnp.logical_and(jnp.logical_and(s, at_q), is_grad == kind))
            out += dot(m, data)
            hm = ones_where(jnp.logical_and(jnp.logical_and(hs, hat_q), h_is_grad == kind))
            hout += dot(hm, data)
    disp_ref[...] = out.astype(BF)
    hrow_ref[...] = hout.astype(BF)


def pack(hot_index, tokens, cotangent, gate, ids_t, slots_t):
    return pl.pallas_call(
        pack_kernel,
        out_shape=(sds((512, 512)), sds((32, 512))),
        in_specs=[SM, VM, VM, VM, VM, VM],
        out_specs=(VM, VM),
        compiler_params=pltpu.CompilerParams(vmem_limit_bytes=LIMIT),
        name="pack_rows",
    )(hot_index, tokens, cotangent, gate, ids_t, slots_t)


class Place:
    def __init__(self):
        self.dp = lax.axis_index("dp")
        self.e = lax.axis_index("expert")
        self.h = self.dp // 4
        self.y = self.dp % 4
        self.z = self.e // 8
        self.x = (self.e // 2) % 4
        self.c = self.e % 2
        self.me = self.h * 32 + self.e
        self.group = self.me // 8

    def at_y(self, y):
        return (self.h * 4 + y, self.e)

    def at_x(self, x):
        return (self.dp, self.z * 8 + x * 2 + self.c)

    def at_z(self, z):
        return (self.dp, z * 8 + self.x * 2 + self.c)

    def partner(self):
        return (self.dp, self.e + 1 - 2 * self.c)

    def at_peer(self, p):
        return ((p // 32) * 4 + self.y, p % 32)


def send(src, dst, ssem, rsem, to):
    copy = pltpu.make_async_remote_copy(
        src_ref=src, dst_ref=dst, send_sem=ssem, recv_sem=rsem, device_id=to, device_id_type=MESH
    )
    copy.start()


def local(src, dst, sem):
    pltpu.make_async_copy(src, dst, sem).start()


def wait(ref, sem):
    pltpu.make_async_copy(ref, ref, sem).wait()


def greet(at):
    barrier = pltpu.get_barrier_semaphore()

    def one(k, _):
        pl.semaphore_signal(
            barrier, inc=1, device_id=at.at_peer((at.me + k) % 64), device_id_type=MESH
        )
        return 0

    lax.fori_loop(1, 64, one, 0)
    for k in range(1, 4):
        pl.semaphore_signal(
            barrier, inc=1, device_id=at.at_y((at.y + k) % 4), device_id_type=MESH
        )
    pl.semaphore_wait(barrier, 66)


def rows(start, size):
    return pl.ds(pl.multiple_of(start, 16), size)


def first_kernel(
    flags, disp, hrow, up, down,
    buf, hbuf, uph, dnh,
    p_up, p_dn, o_up, o_dn, m_up, m_dn, r_up, r_dn, t_up, t_dn,
    disp_s, disp_r, y_s, y_r, y_f, h_s, h_r, hy_s, hy_r,
    s1_s, s1_r, s1_l, s2_s, s2_m, s2_raw, s2_acc, s3_s, s3_r, s4_s, s4_r, s4_l, s5_s, s5_r, s5_f, s6_s, s6_r,
):
    at = Place()
    y, x, z, c = at.y, at.x, at.z, at.c
    yr, yl, yo = (y + 1) % 4, (y + 3) % 4, (y + 2) % 4
    xr, xl, xo = (x + 1) % 4, (x + 3) % 4, (x + 2) % 4
    arrays = ((up, o_up, p_up, 1024), (down, o_dn, p_dn, 256))
    for i, (w, own, _, n) in enumerate(arrays):
        local(w.at[rows(c * n, n)], own, s1_l.at[i])
    greet(at)
    for i, (w, _, other, n) in enumerate(arrays):
        send(w.at[rows((1 - c) * n, n)], other, s1_s.at[i], s1_r.at[i], at.partner())

    def dispatch(k, _):
        p = (at.me + k) % 64
        send(disp.at[p % 32], buf.at[y, at.me], disp_s, disp_r.at[at.group], at.at_peer(p))
        return 0

    local(disp.at[at.e], buf.at[y, at.me], disp_r.at[at.group])
    local(hrow, hbuf.at[y, at.h], h_r.at[0])
    send(hrow, hbuf.at[y, at.h], h_s, h_r.at[1], at.at_peer((at.me + 32) % 64))
    lax.fori_loop(1, 64, dispatch, 0)

    for i, (w, own, other, n) in enumerate(arrays):
        wait(own, s1_l.at[i])
        wait(other, s1_r.at[i])
    f_own, f_other = flags[0], flags[1]
    for own, other, n in ((o_up, p_up, 1024), (o_dn, p_dn, 256)):

        def choose(k, _, own=own, other=other, n=n):
            s = rows(k * (n // 16), n // 16)
            own[s] = (own[s].astype(F32) * f_own + other[s].astype(F32) * f_other).astype(BF)
            return 0

        lax.fori_loop(0, 16, choose, 0)

    ring = ((o_up, m_up, r_up, t_up, 128), (o_dn, m_dn, r_dn, t_dn, 32))
    for i, (o, m, r, t, n) in enumerate(ring):
        send(o.at[rows(xo * 2 * n, n)], m.at[0], s2_s.at[i, 0], s2_m.at[i, 0], at.at_x(xr))
        send(o.at[rows(xo * 2 * n + n, n)], m.at[1], s2_s.at[i, 1], s2_m.at[i, 1], at.at_x(xl))
        send(o.at[rows(xr * 2 * n + n, n)], r.at[0, pl.ds(n, n)], s2_s.at[i, 2], s2_raw.at[i, 0], at.at_x(xr))
        send(o.at[rows(xl * 2 * n, n)], r.at[1, pl.ds(0, n)], s2_s.at[i, 3], s2_raw.at[i, 1], at.at_x(xl))

    groups = [(at.group + off) % 8 for off in Z_OFFSETS]

    def slab(of_y, g):
        return buf.at[of_y, pl.ds(g * 8, 8)]

    def pass_on(i):
        g = groups[i]
        wait(slab(y, g), disp_r.at[g])
        send(slab(y, g), slab(y, g), y_s, y_r.at[0, i], at.at_y(yr))
        send(slab(y, g), slab(y, g), y_s, y_r.at[1, i], at.at_y(yl))

    def forward(i):
        g = groups[i]
        wait(slab(yl, g), y_r.at[0, i])
        if i % 2 == 0:
            send(slab(yl, g), slab(yl, g), y_s, y_f.at[i], at.at_y(yr))
        wait(slab(yr, g), y_r.at[1, i])
        if i % 2 == 1:
            send(slab(yr, g), slab(yr, g), y_s, y_f.at[i], at.at_y(yl))

    for i in range(4):
        pass_on(i)

    for i, (o, m, r, t, n) in enumerate(ring):
        wait(m.at[0], s2_m.at[i, 0])
        m[0] = m[0] + o[rows(xr * 2 * n, n)]
        send(m.at[0], r.at[0, pl.ds(0, n)], s2_s.at[i, 4], s2_acc.at[i, 0], at.at_x(xr))
        wait(m.at[1], s2_m.at[i, 1])
        m[1] = m[1] + o[rows(xl * 2 * n + n, n)]
        send(m.at[1], r.at[1, pl.ds(n, n)], s2_s.at[i, 5], s2_acc.at[i, 1], at.at_x(xl))

    for i in range(4, 8):
        pass_on(i)

    wait(hbuf.at[y, at.h], h_r.at[0])
    wait(hbuf.at[y, 1 - at.h], h_r.at[1])
    for k in range(1, 4):
        send(hbuf.at[y], hbuf.at[y], hy_s, hy_r, at.at_y((y + k) % 4))

    for i, (o, m, r, t, n) in enumerate(ring):
        for side, raw, acc in ((0, pl.ds(n, n), pl.ds(0, n)), (1, pl.ds(0, n), pl.ds(n, n))):
            wait(r.at[side, raw], s2_raw.at[i, side])
            wait(r.at[side, acc], s2_acc.at[i, side])
        r[0] = r[0] + r[1] + o[rows(x * 2 * n, 2 * n)]
        w = n // 2
        for k in range(1, 4):
            zz = (z + k) % 4
            send(r.at[0, rows(zz * w, w)], t.at[k - 1], s3_s.at[i, k - 1], s3_r.at[i, k - 1], at.at_z(zz))

    for i in range(4):
        forward(i)

    full = ((uph, t_up, r_up, 64), (dnh, t_dn, r_dn, 16))
    for i, (dst, t, r, w) in enumerate(full):
        for k in range(3):
            wait(t.at[k], s3_r.at[i, k])
        t[3] = t[0] + t[1] + t[2] + r[0, rows(z * w, w)]
        place = rows(c * 16 * w + x * 4 * w + z * w, w)
        local(t.at[3], dst.at[place], s4_l.at[i])
        for k in range(1, 4):
            send(t.at[3], dst.at[place], s4_s.at[i, k - 1], s4_r.at[i, k - 1], at.at_z((z + k) % 4))

    for i in range(4, 8):
        forward(i)

    for i, (dst, t, r, w) in enumerate(full):
        wait(t.at[3], s4_l.at[i])
        for k in range(3):
            wait(t.at[3], s4_r.at[i, k])

        def half(xx, b, dst=dst, w=w):
            return dst.at[rows(c * 16 * w + xx * 4 * w + b * 2 * w, 2 * w)]

        for b in range(2):
            send(half(x, b), half(x, b), s5_s.at[i, b], s5_r.at[i, 0, b], at.at_x(xr))
            send(half(x, b), half(x, b), s5_s.at[i, 2 + b], s5_r.at[i, 1, b], at.at_x(xl))
        quarter = dst.at[rows(c * 16 * w + x * 4 * w, 4 * w)]
        send(quarter, quarter, s6_s.at[i, 0], s6_r.at[i, 0], at.partner())
    for i, (dst, t, r, w) in enumerate(full):

        def half(xx, b, dst=dst, w=w):
            return dst.at[rows(c * 16 * w + xx * 4 * w + b * 2 * w, 2 * w)]

        wait(half(xl, 0), s5_r.at[i, 0, 0])
        send(half(xl, 0), half(xl, 0), s5_s.at[i, 4], s5_f.at[i, 0], at.at_x(xr))
        wait(half(xr, 1), s5_r.at[i, 1, 1])
        send(half(xr, 1), half(xr, 1), s5_s.at[i, 5], s5_f.at[i, 1], at.at_x(xl))
    for i, (dst, t, r, w) in enumerate(full):

        def half(xx, b, dst=dst, w=w):
            return dst.at[rows(c * 16 * w + xx * 4 * w + b * 2 * w, 2 * w)]

        wait(half(xl, 1), s5_r.at[i, 0, 1])
        wait(half(xr, 0), s5_r.at[i, 1, 0])
        for k, xx in ((1, xl), (2, xr)):
            quarter = dst.at[rows(c * 16 * w + xx * 4 * w, 4 * w)]
            send(quarter, quarter, s6_s.at[i, k], s6_r.at[i, k], at.partner())
    for i, (dst, t, r, w) in enumerate(full):

        def half(xx, b, dst=dst, w=w):
            return dst.at[rows(c * 16 * w + xx * 4 * w + b * 2 * w, 2 * w)]

        wait(half(xo, 0), s5_f.at[i, 0])
        wait(half(xo, 1), s5_f.at[i, 1])
        quarter = dst.at[rows(c * 16 * w + xo * 4 * w, 4 * w)]
        send(quarter, quarter, s6_s.at[i, 3], s6_r.at[i, 3], at.partner())

    for i in range(8):
        wait(slab(yo, groups[i]), y_f.at[i])
    wait(hbuf.at[pl.ds(0, 3)], hy_r)
    for i, (w, own, other, n) in enumerate(arrays):
        wait(own, s1_s.at[i])
    wait(buf.at[0, pl.ds(0, 63)], disp_s)
    wait(buf.at[pl.ds(0, 3)], y_s)
    wait(hbuf.at[pl.ds(0, 3)], hy_s)
    wait(hbuf.at[0, 0], h_s)
    for i, (o, m, r, t, n) in enumerate(ring):
        for k in range(6):
            wait(m.at[0], s2_s.at[i, k])
        for k in range(3):
            wait(t.at[0], s3_s.at[i, k])
            wait(t.at[0], s4_s.at[i, k])
    for i, (dst, t, r, w) in enumerate(full):
        for k in range(6):
            wait(dst.at[pl.ds(0, 2 * w)], s5_s.at[i, k])
        for k in range(4):
            wait(dst.at[pl.ds(0, 4 * w)], s6_s.at[i, k])
            wait(dst.at[pl.ds(0, 4 * w)], s6_r.at[i, k])


def first_exchange(flags, disp, hrow, up, down):
    return pl.pallas_call(
        first_kernel,
        out_shape=(sds((4, 64, 16, 512)), sds((4, 2, 32, 512)), sds((2048, 512)), sds((512, 2048))),
        in_specs=[SM, ANY, ANY, ANY, ANY],
        out_specs=(ANY, ANY, ANY, ANY),
        scratch_shapes=[
            pltpu.VMEM((1024, 512), BF),
            pltpu.VMEM((256, 2048), BF),
            pltpu.VMEM((1024, 512), BF),
            pltpu.VMEM((256, 2048), BF),
            pltpu.VMEM((2, 128, 512), BF),
            pltpu.VMEM((2, 32, 2048), BF),
            pltpu.VMEM((2, 256, 512), BF),
            pltpu.VMEM((2, 64, 2048), BF),
            pltpu.VMEM((4, 64, 512), BF),
            pltpu.VMEM((4, 16, 2048), BF),
            DMA, DMA((8,)), DMA, DMA((2, 8)), DMA((8,)), DMA, DMA((2,)), DMA, DMA,
            DMA((2,)), DMA((2,)), DMA((2,)),
            DMA((2, 6)), DMA((2, 2)), DMA((2, 2)), DMA((2, 2)),
            DMA((2, 3)), DMA((2, 3)), DMA((2, 3)), DMA((2, 3)), DMA((2,)),
            DMA((2, 6)), DMA((2, 2, 2)), DMA((2, 2)), DMA((2, 4)), DMA((2, 4)),
        ],
        compiler_params=pltpu.CompilerParams(
            collective_id=1, has_side_effects=True, vmem_limit_bytes=32 * 1024 * 1024
        ),
        name="first_exchange",
    )(flags, disp, hrow, up, down)


def gelu_pair(preact):
    normal_cdf = 0.5 * (1.0 + lax.erf(preact * 0.7071067811865476))
    density = jnp.exp(-0.5 * preact * preact) * 0.3989422804014327
    return (preact * normal_cdf, normal_cdf + preact * density)


def order_matrix(src_count, slot_count):
    r = iota((256, 256), 0)
    k = iota((256, 256), 1)
    slot = r % slot_count
    src = (r // slot_count) % src_count
    q = (r // 32) % 4
    a = r // 128
    return ones_where(k == src * (8 * slot_count) + a * (4 * slot_count) + slot * 4 + q)


def expert_kernel(
    buf, up, down, hbuf, uph, dnh, gu, gd, parts, hparts, apack, wsend, xs, act_s, pre_s, ys
):
    order = order_matrix(16, 2)

    def sort_rows(b, _):
        block = dot(order, buf[rows(b * 256, 256)]).astype(BF)
        for k in range(8):
            xs[k, rows(b * 32, 32)] = block[k * 32 : (k + 1) * 32]
        return 0

    lax.fori_loop(0, 16, sort_rows, 0)

    def hidden(b, _):
        s = rows(b * 128, 128)
        preact = dot(xs[0, s], up[0:512])
        dact = dot_nt(xs[4, s], down[:, 0:512])
        for q in range(1, 4):
            preact += dot(xs[q, s], up[q * 512 : (q + 1) * 512])
            dact += dot_nt(xs[4 + q, s], down[:, q * 512 : (q + 1) * 512])
        value, slope = gelu_pair(preact)
        act_s[s] = value.astype(BF)
        pre_s[s] = (dact * slope).astype(BF)
        return 0

    lax.fori_loop(0, 4, hidden, 0)

    for q in range(4):
        cols = slice(q * 512, (q + 1) * 512)
        gu[cols, :] = dot_tn(xs[q], pre_s[...]).astype(BF)
        gd[cols, :] = dot_tn(xs[4 + q], act_s[...]).astype(BF)
        ys[q] = dot(act_s[...], down[:, cols]).astype(BF)
        ys[4 + q] = dot_nt(pre_s[...], up[cols, :]).astype(BF)

    def unsort_rows(b, _):
        block = jnp.concatenate([ys[k, rows(b * 32, 32)] for k in range(8)], axis=0)
        parts[rows(b * 256, 256)] = dot_tn(order, block).astype(BF)
        return 0

    lax.fori_loop(0, 16, unsort_rows, 0)

    horder = order_matrix(8, 4)
    hx = dot(horder, hbuf[...]).astype(BF)
    hx = [hx[k * 32 : (k + 1) * 32] for k in range(8)]
    preact = dot(hx[0], uph[0:512])
    dact = dot_nt(hx[4], dnh[:, 0:512])
    for q in range(1, 4):
        preact += dot(hx[q], uph[q * 512 : (q + 1) * 512])
        dact += dot_nt(hx[4 + q], dnh[:, q * 512 : (q + 1) * 512])
    value, slope = gelu_pair(preact)
    hact = value.astype(BF)
    hpre = (dact * slope).astype(BF)
    apack[:, 0:512] = hpre
    apack[:, 512:1024] = hact
    outs = [dot(hact, dnh[:, q * 512 : (q + 1) * 512]).astype(BF) for q in range(4)]
    backs = [dot_nt(hpre, uph[q * 512 : (q + 1) * 512, :]).astype(BF) for q in range(4)]
    hparts[...] = dot_tn(horder, jnp.concatenate(outs + backs, axis=0)).astype(BF)
    i = iota((128, 128), 0)
    j = iota((128, 128), 1)
    for odd in range(2):
        take_in = ones_where(jnp.logical_and(j < 64, i == j + 64 * odd))
        take_grad = ones_where(jnp.logical_and(j >= 64, i == j - 64 + 64 * odd))
        for b in range(16):
            q, o = b // 4, (b % 4) * 128
            block = dot(hx[q][:, o : o + 128], take_in) + dot(hx[4 + q][:, o : o + 128], take_grad)
            wsend[2 * b + odd] = block.astype(BF)


def experts(buf, up, down, hbuf, uph, dnh):
    return pl.pallas_call(
        expert_kernel,
        out_shape=(
            sds((2048, 512)), sds((2048, 512)), sds((4096, 512)), sds((256, 512)),
            sds((32, 1024)), sds((32, 32, 128)),
        ),
        in_specs=[VM] * 6,
        out_specs=(VM,) * 6,
        scratch_shapes=[
            pltpu.VMEM((8, 512, 512), BF),
            pltpu.VMEM((512, 512), BF),
            pltpu.VMEM((512, 512), BF),
            pltpu.VMEM((8, 512, 512), BF),
        ],
        compiler_params=pltpu.CompilerParams(vmem_limit_bytes=LIMIT),
        name="experts",
    )(buf, up, down, hbuf, uph, dnh)


def second_kernel(
    gu, gd, parts, hparts, apack, wsend,
    ogu, ogd, rbuf, rhot, apool, wrecv,
    m, r, ret, hr, hret,
    g_s, g_r, w_s, w_r, m_s, m_r, raw_s, raw_r, acc_s, acc_r, ret_s, ret_r,
    hp_s, hp_r, hret_s, hret_r, az_s, az_r, ax_s, ax_r, ac_s, ac_r,
):
    at = Place()
    y, x, z, c = at.y, at.x, at.z, at.c
    yr, yl, yo = (y + 1) % 4, (y + 3) % 4, (y + 2) % 4
    greet(at)

    def part(of_y, g):
        return parts.at[of_y, pl.ds(g * 8, 8)]

    for i in range(4):
        send(part(yo, i), m.at[0, i], m_s, m_r.at[0, i], at.at_y(yr))
        send(part(yo, 4 + i), m.at[1, i], m_s, m_r.at[1, i], at.at_y(yl))
    for i in range(4):
        send(part(yr, 4 + i), r.at[0, 4 + i], raw_s, raw_r.at[0, i], at.at_y(yr))
        send(part(yl, i), r.at[1, i], raw_s, raw_r.at[1, i], at.at_y(yl))
    for k in range(1, 4):
        yy = (y + k) % 4
        send(hparts.at[yy], hr.at[k - 1], hp_s, hp_r.at[k - 1], at.at_y(yy))
    local(apack, apool.at[z, x, c], az_r.at[3])
    for k in range(1, 4):
        send(apack, apool.at[z, x, c], az_s, az_r.at[k - 1], at.at_z((z + k) % 4))

    def gradients(k, _):
        e = (at.e + k) % 32
        to = (at.dp, e)
        send(gu.at[pl.ds(e * 64, 64)], ogu.at[at.e], g_s.at[0], g_r.at[0], to)
        send(gd.at[pl.ds(e * 64, 64)], ogd.at[at.e], g_s.at[1], g_r.at[1], to)
        return 0

    def widths(k, _):
        e = (at.e + k) % 32
        send(wsend.at[e], wrecv.at[at.e], w_s, w_r, (at.dp, e))
        return 0

    local(gu.at[rows(at.e * 64, 64)], ogu.at[at.e], g_r.at[0])
    local(gd.at[rows(at.e * 64, 64)], ogd.at[at.e], g_r.at[1])
    local(wsend.at[at.e], wrecv.at[at.e], w_r)
    lax.fori_loop(1, 32, gradients, 0)
    lax.fori_loop(1, 32, widths, 0)

    for i in range(4):
        wait(m.at[0, i], m_r.at[0, i])
        m[0, i] = (m[0, i].astype(F32) + parts[yr, pl.ds(i * 8, 8)].astype(F32)).astype(BF)
        send(m.at[0, i], r.at[0, i], acc_s, acc_r.at[0, i], at.at_y(yr))
        wait(m.at[1, i], m_r.at[1, i])
        m[1, i] = (m[1, i].astype(F32) + parts[yl, pl.ds(32 + i * 8, 8)].astype(F32)).astype(BF)
        send(m.at[1, i], r.at[1, 4 + i], acc_s, acc_r.at[1, i], at.at_y(yl))

    for k in range(4):
        wait(apack, az_r.at[k])
    for k in range(1, 4):
        send(apool.at[:, x, c], apool.at[:, x, c], ax_s, ax_r.at[k - 1], at.at_x((x + k) % 4))
    for k in range(3):
        wait(hr.at[k], hp_r.at[k])
    hret[...] = (
        hparts[y].astype(F32) + hr[0].astype(F32) + hr[1].astype(F32) + hr[2].astype(F32)
    ).astype(BF)
    local(hret.at[at.h], rhot.at[at.h], hret_r.at[0])
    send(hret.at[1 - at.h], rhot.at[at.h], hret_s, hret_r.at[1], at.at_peer((at.me + 32) % 64))

    for i in range(8):
        side_raw, side_acc = (1, 0) if i < 4 else (0, 1)
        wait(r.at[side_raw, i], raw_r.at[side_raw, i % 4])
        wait(r.at[side_acc, i], acc_r.at[side_acc, i % 4])
        ret[pl.ds(i * 8, 8)] = (
            parts[y, pl.ds(i * 8, 8)].astype(F32) + r[0, i].astype(F32) + r[1, i].astype(F32)
        ).astype(BF)

        def give_back(j, _, i=i):
            p = i * 8 + j

            @pl.when(p != at.me)
            def _():
                send(ret.at[p], rbuf.at[at.me], ret_s, ret_r, at.at_peer(p))

            @pl.when(p == at.me)
            def _():
                local(ret.at[p], rbuf.at[p], ret_r)

            return 0

        lax.fori_loop(0, 8, give_back, 0)

    for k in range(3):
        wait(apool.at[:, 0, 0], ax_r.at[k])
    send(apool.at[:, :, c], apool.at[:, :, c], ac_s, ac_r, at.partner())

    wait(ogu, g_r.at[0])
    wait(ogd, g_r.at[1])
    wait(wrecv, w_r)
    wait(rbuf, ret_r)
    wait(rhot.at[0], hret_r.at[0])
    wait(rhot.at[0], hret_r.at[1])
    wait(apool.at[:, :, 0], ac_r)
    wait(gu.at[pl.ds(0, 31 * 64)], g_s.at[0])
    wait(gd.at[pl.ds(0, 31 * 64)], g_s.at[1])
    wait(wsend.at[pl.ds(0, 31)], w_s)
    wait(m, m_s)
    wait(m, raw_s)
    wait(m, acc_s)
    wait(ret.at[pl.ds(0, 63)], ret_s)
    wait(hr, hp_s)
    wait(hret.at[0], hret_s)
    wait(apool.at[0, 0:3, 0], az_s)
    wait(apool.at[:, 0:3, 0], ax_s)
    wait(apool.at[:, :, 0], ac_s)


def second_exchange(gu, gd, parts, hparts, apack, wsend):
    return pl.pallas_call(
        second_kernel,
        out_shape=(
            sds((32, 64, 512)), sds((32, 64, 512)), sds((64, 16, 512)), sds((2, 32, 512)),
            sds((4, 4, 2, 32, 1024)), sds((32, 32, 128)),
        ),
        in_specs=[ANY, ANY, VM, VM, ANY, ANY],
        out_specs=(ANY,) * 6,
        scratch_shapes=[
            pltpu.VMEM((2, 4, 8, 16, 512), BF),
            pltpu.VMEM((2, 8, 8, 16, 512), BF),
            pltpu.VMEM((64, 16, 512), BF),
            pltpu.VMEM((3, 2, 32, 512), BF),
            pltpu.VMEM((2, 32, 512), BF),
            DMA((2,)), DMA((2,)), DMA, DMA, DMA, DMA((2, 4)), DMA, DMA((2, 4)), DMA, DMA((2, 4)), DMA, DMA,
            DMA, DMA((3,)), DMA, DMA((2,)), DMA, DMA((4,)), DMA, DMA((3,)), DMA, DMA,
        ],
        compiler_params=pltpu.CompilerParams(
            collective_id=2, has_side_effects=True, vmem_limit_bytes=32 * 1024 * 1024
        ),
        name="second_exchange",
    )(gu, gd, parts, hparts, apack, wsend)


def combine_kernel(hot_ref, rbuf, rhot, gate_ref, ids_ref, slots_ref, wrecv, apool, out_ref, back_ref, hup_ref, hdn_ref):
    hot = hot_ref[0]
    r = iota((128, 1024), 1)
    code = ((r // 16) % 32) * CAP + (r // 4) % 2
    is_back = (r // 8) % 2
    quarter = r % 4
    hr = iota((128, 64), 1)
    hcode = (hr // 4) % 4
    h_is_back = (hr // 16) % 2
    hquarter = hr % 4
    sel, hsel = [], []
    for c in range(2):
        ids = ids_ref[:, c : c + 1]
        slot = slots_ref[:, c : c + 1]
        is_hot = ids == hot
        place = jnp.where(jnp.logical_and(jnp.logical_not(is_hot), slot < CAP), ids * CAP + slot, -1)
        hplace = jnp.where(jnp.logical_and(is_hot, slot < HCAP), slot, -1)
        sel.append(code == place)
        hsel.append(hcode == hplace)
    data = rbuf[...]
    hdata = rhot[...]

    def pick(s, hs, q, kind):
        m = ones_where(jnp.logical_and(jnp.logical_and(s, quarter == q), is_back == kind))
        hm = ones_where(jnp.logical_and(jnp.logical_and(hs, hquarter == q), h_is_back == kind))
        return dot(m, data) + dot(hm, hdata)

    either = jnp.logical_or(sel[0], sel[1])
    heither = jnp.logical_or(hsel[0], hsel[1])
    for q in range(4):
        cols = slice(q * 512, (q + 1) * 512)
        out = gate_ref[:, 0:1] * pick(sel[0], hsel[0], q, 0) + gate_ref[:, 1:2] * pick(sel[1], hsel[1], q, 0)
        out_ref[:, cols] = out.astype(BF)
        back_ref[:, cols] = pick(either, heither, q, 1).astype(BF)
    w = wrecv[...]
    hup_ref[...] = dot_tn(w, apool[:, 0:512])[0:64]
    hdn_ref[...] = dot_tn(w, apool[:, 512:1024])[64:128]


def combine(hot_index, rbuf, rhot, gate, ids, slots, wrecv, apool):
    return pl.pallas_call(
        combine_kernel,
        out_shape=(sds((128, 2048)), sds((128, 2048)), sds((64, 512), F32), sds((64, 512), F32)),
        in_specs=[SM] + [VM] * 7,
        out_specs=(VM,) * 4,
        compiler_params=pltpu.CompilerParams(vmem_limit_bytes=LIMIT),
        name="combine",
    )(hot_index, rbuf, rhot, gate, ids, slots, wrecv, apool)


def on_device(tokens, cotangent, gate_probs, expert_ids, route_slots, hot_mask, w_up, w_down):
    up, down = w_up[0], w_down[0]
    codes = jnp.arange(hot_mask.shape[0], dtype=jnp.int32)
    hot_index = jnp.sum(hot_mask * codes).reshape(1)
    me = lax.axis_index("expert")
    partner = me + 1 - 2 * (me % 2)
    flags = jnp.stack([hot_index[0] == me, hot_index[0] == partner]).astype(F32)
    disp, hrow = pack(hot_index, tokens, cotangent, gate_probs, expert_ids.T, route_slots.T)
    buf, hbuf, uph, dnh = first_exchange(flags, disp.reshape(32, 16, 512), hrow, up, down)
    gu, gd, parts, hparts, apack, wsend = experts(
        buf.reshape(4096, 512), up, down, hbuf.reshape(256, 512), uph, dnh
    )
    ogu, ogd, rbuf, rhot, apool, wrecv = second_exchange(
        gu, gd, parts.reshape(4, 64, 16, 512), hparts.reshape(4, 2, 32, 512), apack, wsend
    )
    layer_out, grad_tokens, hup, hdn = combine(
        hot_index, rbuf.reshape(1024, 512), rhot.reshape(64, 512), gate_probs, expert_ids, route_slots,
        wrecv.reshape(1024, 128), apool.reshape(1024, 1024),
    )
    is_hot = (hot_mask > 0)[:, None, None]
    grad_up = jnp.where(is_hot, hup.astype(BF)[None], ogu)
    grad_down = jnp.where(is_hot, hdn.astype(BF)[None], ogd)
    return (layer_out, grad_tokens, grad_up, grad_down)


def solution(mesh):
    placed = (
        P(("dp", "expert"), None),
        P(("dp", "expert"), None),
        P(("dp", "expert"), None),
        P(("dp", "expert"), None),
        P(("dp", "expert"), None),
        P(),
        P("expert", None, "dp"),
        P("expert", "dp", None),
    )
    return jax.shard_map(
        on_device,
        mesh=mesh,
        in_specs=placed,
        out_specs=(
            P(("dp", "expert"), None),
            P(("dp", "expert"), None),
            P(None, "expert", "dp"),
            P(None, "expert", "dp"),
        ),
        check_vma=False,
    )
```

```python
import functools

import jax
import jax.numpy as jnp
from jax import lax
from jax.experimental import pallas as pl
from jax.experimental.pallas import tpu as pltpu
from jax.sharding import PartitionSpec as P

CAP = 2
HCAP = 4
MESH = pl.DeviceIdType.MESH
BF = jnp.bfloat16
F32 = jnp.float32
ANY = pl.BlockSpec(memory_space=pl.ANY)
VM = pl.BlockSpec(memory_space=pltpu.VMEM)
SM = pl.BlockSpec(memory_space=pltpu.SMEM)
DMA = pltpu.SemaphoreType.DMA
Z_OFFSETS = (0, 1, 7, 2, 6, 3, 5, 4)
LIMIT = 60 * 1024 * 1024


def sds(shape, dtype=BF):
    return jax.ShapeDtypeStruct(shape, dtype)


def iota(shape, dim):
    return lax.broadcasted_iota(jnp.int32, shape, dim)


def dot(a, b):
    return jnp.dot(a, b, preferred_element_type=F32)


def dot_nt(a, b):
    return lax.dot_general(a, b, (((1,), (1,)), ((), ())), preferred_element_type=F32)


def dot_tn(a, b):
    return lax.dot_general(a, b, (((0,), (0,)), ((), ())), preferred_element_type=F32)


def ones_where(cond):
    return jnp.where(cond, 1.0, 0.0).astype(BF)


class Place:
    def __init__(self):
        self.dp = lax.axis_index("dp")
        self.e = lax.axis_index("expert")
        self.h = self.dp // 4
        self.y = self.dp % 4
        self.z = self.e // 8
        self.x = (self.e // 2) % 4
        self.c = self.e % 2
        self.me = self.h * 32 + self.e
        self.group = self.me // 8

    def at_y(self, y):
        return (self.h * 4 + y, self.e)

    def at_x(self, x):
        return (self.dp, self.z * 8 + x * 2 + self.c)

    def at_z(self, z):
        return (self.dp, z * 8 + self.x * 2 + self.c)

    def partner(self):
        return (self.dp, self.e + 1 - 2 * self.c)

    def at_peer(self, p):
        return ((p // 32) * 4 + self.y, p % 32)


def send(src, dst, ssem, rsem, to):
    copy = pltpu.make_async_remote_copy(
        src_ref=src, dst_ref=dst, send_sem=ssem, recv_sem=rsem, device_id=to, device_id_type=MESH
    )
    copy.start()


def local(src, dst, sem):
    pltpu.make_async_copy(src, dst, sem).start()


def wait(ref, sem):
    pltpu.make_async_copy(ref, ref, sem).wait()


def rows(start, size):
    return pl.ds(pl.multiple_of(start, 16), size)


def gelu_pair(preact):
    normal_cdf = 0.5 * (1.0 + lax.erf(preact * 0.7071067811865476))
    density = jnp.exp(-0.5 * preact * preact) * 0.3989422804014327
    return (preact * normal_cdf, normal_cdf + preact * density)


def order_matrix(src_count, slot_count):
    r = iota((256, 256), 0)
    k = iota((256, 256), 1)
    slot = r % slot_count
    src = (r // slot_count) % src_count
    q = (r // 32) % 4
    a = r // 128
    return ones_where(k == src * (8 * slot_count) + a * (4 * slot_count) + slot * 4 + q)


def to_column(row):
    wide = row.shape[1]
    same = iota((wide, wide), 0) == iota((wide, wide), 1)
    return jnp.sum(jnp.where(same, row, jnp.zeros_like(row)), axis=1, keepdims=True)


def places_of(ids, slot, hot):
    is_hot = ids == hot
    normal = jnp.where(jnp.logical_and(jnp.logical_not(is_hot), slot < CAP), ids * CAP + slot, -1)
    special = jnp.where(jnp.logical_and(is_hot, slot < HCAP), slot, -1)
    return normal, special


def pack_rows(hot, tokens, cot, gate_cols, ids, slots, disp, hrow):
    r = iota((512, 128), 0)
    code = (r // 16) * CAP + (r // 4) % 2
    is_grad = (r // 8) % 2
    quarter = r % 4
    hr = iota((32, 128), 0)
    hcode = (hr // 4) % 4
    h_is_grad = hr // 16
    hquarter = hr % 4
    sel, hsel = [], []
    for k in range(2):
        normal, special = places_of(ids[k : k + 1, :], slots[k : k + 1, :], hot)
        sel.append(code == normal)
        hsel.append(hcode == special)
    either = jnp.logical_or(sel[0], sel[1])
    heither = jnp.logical_or(hsel[0], hsel[1])
    out = jnp.zeros((512, 512), F32)
    hout = jnp.zeros((32, 512), F32)
    for q in range(4):
        cols = slice(q * 512, (q + 1) * 512)
        wide = cot[:, cols].astype(F32)
        parts = (
            (tokens[:, cols], either, heither, 0),
            ((gate_cols[0] * wide).astype(BF), sel[0], hsel[0], 1),
            ((gate_cols[1] * wide).astype(BF), sel[1], hsel[1], 1),
        )
        for data, s, hs, kind in parts:
            m = ones_where(jnp.logical_and(jnp.logical_and(s, quarter == q), is_grad == kind))
            out += dot(m, data)
            hm = ones_where(jnp.logical_and(jnp.logical_and(hs, hquarter == q), h_is_grad == kind))
            hout += dot(hm, data)
    disp[...] = out.astype(BF).reshape(32, 16, 512)
    hrow[...] = hout.astype(BF)


def combine_rows(hot, rbuf, rhot, gate_cols, id_cols, slot_cols, out_ref, back_ref):
    r = iota((128, 1024), 1)
    code = ((r // 16) % 32) * CAP + (r // 4) % 2
    is_back = (r // 8) % 2
    quarter = r % 4
    hr = iota((128, 64), 1)
    hcode = (hr // 4) % 4
    h_is_back = (hr // 16) % 2
    hquarter = hr % 4
    sel, hsel = [], []
    for k in range(2):
        normal, special = places_of(id_cols[k], slot_cols[k], hot)
        sel.append(code == normal)
        hsel.append(hcode == special)
    data = rbuf[...].reshape(1024, 512)
    hdata = rhot[...].reshape(64, 512)

    def pick(s, hs, q, kind):
        m = ones_where(jnp.logical_and(jnp.logical_and(s, quarter == q), is_back == kind))
        hm = ones_where(jnp.logical_and(jnp.logical_and(hs, hquarter == q), h_is_back == kind))
        return dot(m, data) + dot(hm, hdata)

    either = jnp.logical_or(sel[0], sel[1])
    heither = jnp.logical_or(hsel[0], hsel[1])
    for q in range(4):
        cols = slice(q * 512, (q + 1) * 512)
        out = gate_cols[0] * pick(sel[0], hsel[0], q, 0) + gate_cols[1] * pick(sel[1], hsel[1], q, 0)
        out_ref[:, cols] = out.astype(BF)
        back_ref[:, cols] = pick(either, heither, q, 1).astype(BF)


def layer_kernel(
    mask_ref, tokens, cot, gate_ref, ids_ref, slots_ref, up, down,
    out_ref, back_ref, hup_ref, hdn_ref, ogu, ogd,
    disp, hrow, buf, hbuf, upv, dnv, uph, dnh,
    p_up, p_dn, o_up, o_dn, m_up, m_dn, r_up, r_dn, t_up, t_dn,
    xs, act_s, pre_s, ys, gu, gd, parts, hparts, apack, wsend,
    m, r, ret, rbuf, hr, hret, rhot, apool, wrecv,
    load_s, disp_s, disp_r, y_s, y_r, y_f, h_s, h_r, hy_s, hy_r,
    s1_s, s1_r, s1_l, s2_s, s2_m, s2_raw, s2_acc, s3_s, s3_r, s4_s, s4_r, s4_l, s5_s, s5_r, s5_f, s6_s, s6_r,
    g_s, g_r, w_s, w_r, m_s, m_r, raw_s, raw_r, acc_s, acc_r, ret_s, ret_r,
    hp_s, hp_r, hret_s, hret_r, az_s, az_r, ax_s, ax_r, ac_s, ac_r,
):
    at = Place()
    y, x, z, c = at.y, at.x, at.z, at.c
    yr, yl, yo = (y + 1) % 4, (y + 3) % 4, (y + 2) % 4
    xr, xl, xo = (x + 1) % 4, (x + 3) % 4, (x + 2) % 4

    barrier = pltpu.get_barrier_semaphore()

    def greet(k, _):
        pl.semaphore_signal(barrier, inc=1, device_id=at.at_peer((at.me + k) % 64), device_id_type=MESH)
        return 0

    lax.fori_loop(1, 64, greet, 0)
    for k in range(1, 4):
        pl.semaphore_signal(barrier, inc=1, device_id=at.at_y((y + k) % 4), device_id_type=MESH)

    arrays = ((up, o_up, p_up, 1024), (down, o_dn, p_dn, 256))
    for i, (w, own, _, n) in enumerate(arrays):
        local(w.at[rows(c * n, n)], own, s1_l.at[i])
    local(up, upv, load_s.at[0])
    local(down, dnv, load_s.at[1])

    hot = mask_ref[0] * 0
    for k in range(1, 32):
        hot += mask_ref[k] * k
    f_own = jnp.where(hot == at.e, 1.0, 0.0)
    f_other = jnp.where(hot == at.e + 1 - 2 * c, 1.0, 0.0)
    gate_cols = [to_column(gate_ref[k : k + 1, :]) for k in range(2)]
    pack_rows(hot, tokens, cot, gate_cols, ids_ref, slots_ref, disp, hrow)

    pl.semaphore_wait(barrier, 66)

    for i, (w, _, other, n) in enumerate(arrays):
        send(w.at[rows((1 - c) * n, n)], other, s1_s.at[i], s1_r.at[i], at.partner())

    local(disp.at[at.e], buf.at[y, at.me], disp_r.at[at.group])
    groups = [(at.group + off) % 8 for off in Z_OFFSETS]
    for i, off in enumerate(Z_OFFSETS):

        def dispatch(k, _, g=groups[i]):
            p = g * 8 + (at.me + k) % 8
            send(disp.at[p % 32], buf.at[y, at.me], disp_s, disp_r.at[at.group], at.at_peer(p))
            return 0

        lax.fori_loop(1 if i == 0 else 0, 8, dispatch, 0)
    local(hrow, hbuf.at[y, at.h], h_r.at[0])
    send(hrow, hbuf.at[y, at.h], h_s, h_r.at[1], at.at_peer((at.me + 32) % 64))

    for i, (w, own, other, n) in enumerate(arrays):
        wait(own, s1_l.at[i])
        wait(other, s1_r.at[i])
    for own, other, n in ((o_up, p_up, 1024), (o_dn, p_dn, 256)):

        def choose(k, _, own=own, other=other, n=n):
            s = rows(k * (n // 16), n // 16)
            own[s] = (own[s].astype(F32) * f_own + other[s].astype(F32) * f_other).astype(BF)
            return 0

        lax.fori_loop(0, 16, choose, 0)

    ring = ((o_up, m_up, r_up, t_up, 128), (o_dn, m_dn, r_dn, t_dn, 32))
    for i, (o, mm, rr, t, n) in enumerate(ring):
        send(o.at[rows(xo * 2 * n, n)], mm.at[0], s2_s.at[i, 0], s2_m.at[i, 0], at.at_x(xr))
        send(o.at[rows(xo * 2 * n + n, n)], mm.at[1], s2_s.at[i, 1], s2_m.at[i, 1], at.at_x(xl))
        send(o.at[rows(xr * 2 * n + n, n)], rr.at[0, pl.ds(n, n)], s2_s.at[i, 2], s2_raw.at[i, 0], at.at_x(xr))
        send(o.at[rows(xl * 2 * n, n)], rr.at[1, pl.ds(0, n)], s2_s.at[i, 3], s2_raw.at[i, 1], at.at_x(xl))

    def slab(of_y, g):
        return buf.at[of_y, pl.ds(g * 8, 8)]

    def pass_on(i):
        g = groups[i]
        wait(slab(y, g), disp_r.at[g])
        send(slab(y, g), slab(y, g), y_s, y_r.at[0, i], at.at_y(yr))
        send(slab(y, g), slab(y, g), y_s, y_r.at[1, i], at.at_y(yl))

    def forward(i):
        g = groups[i]
        wait(slab(yl, g), y_r.at[0, i])
        if i % 2 == 0:
            send(slab(yl, g), slab(yl, g), y_s, y_f.at[i], at.at_y(yr))
        wait(slab(yr, g), y_r.at[1, i])
        if i % 2 == 1:
            send(slab(yr, g), slab(yr, g), y_s, y_f.at[i], at.at_y(yl))

    order = order_matrix(16, 2)

    def hidden(s):
        def sort_rows(b, _):
            data = buf[s, pl.ds(b * 16, 16)].reshape(256, 512)
            block = dot(order, data).astype(BF)
            for k in range(8):
                xs[k, rows(s * 128 + b * 32, 32)] = block[k * 32 : (k + 1) * 32]
            return 0

        lax.fori_loop(0, 4, sort_rows, 0)
        at_s = rows(s * 128, 128)
        preact = dot(xs[0, at_s], upv[0:512])
        dact = dot_nt(xs[4, at_s], dnv[:, 0:512])
        for q in range(1, 4):
            preact += dot(xs[q, at_s], upv[q * 512 : (q + 1) * 512])
            dact += dot_nt(xs[4 + q, at_s], dnv[:, q * 512 : (q + 1) * 512])
        value, slope = gelu_pair(preact)
        act_s[at_s] = value.astype(BF)
        pre_s[at_s] = (dact * slope).astype(BF)

    for i in range(5):
        pass_on(i)

    for i, (o, mm, rr, t, n) in enumerate(ring):
        wait(mm.at[0], s2_m.at[i, 0])
        mm[0] = mm[0] + o[rows(xr * 2 * n, n)]
        send(mm.at[0], rr.at[0, pl.ds(0, n)], s2_s.at[i, 4], s2_acc.at[i, 0], at.at_x(xr))
        wait(mm.at[1], s2_m.at[i, 1])
        mm[1] = mm[1] + o[rows(xl * 2 * n + n, n)]
        send(mm.at[1], rr.at[1, pl.ds(n, n)], s2_s.at[i, 5], s2_acc.at[i, 1], at.at_x(xl))

    for i in range(5, 8):
        pass_on(i)

    wait(hbuf.at[y, at.h], h_r.at[0])
    wait(hbuf.at[y, 1 - at.h], h_r.at[1])
    for k in range(1, 4):
        send(hbuf.at[y], hbuf.at[y], hy_s, hy_r, at.at_y((y + k) % 4))

    for i in range(2):
        forward(i)
    wait(upv, load_s.at[0])
    wait(dnv, load_s.at[1])
    hidden(y)
    for i in range(2, 4):
        forward(i)

    for i, (o, mm, rr, t, n) in enumerate(ring):
        for side, raw, acc in ((0, pl.ds(n, n), pl.ds(0, n)), (1, pl.ds(0, n), pl.ds(n, n))):
            wait(rr.at[side, raw], s2_raw.at[i, side])
            wait(rr.at[side, acc], s2_acc.at[i, side])
        rr[0] = rr[0] + rr[1] + o[rows(x * 2 * n, 2 * n)]
        w = n // 2
        for k in range(1, 4):
            zz = (z + k) % 4
            send(rr.at[0, rows(zz * w, w)], t.at[k - 1], s3_s.at[i, k - 1], s3_r.at[i, k - 1], at.at_z(zz))

    for i in range(4, 8):
        forward(i)

    full = ((uph, t_up, r_up, 64), (dnh, t_dn, r_dn, 16))
    for i, (dst, t, rr, w) in enumerate(full):
        for k in range(3):
            wait(t.at[k], s3_r.at[i, k])
        t[3] = t[0] + t[1] + t[2] + rr[0, rows(z * w, w)]
        place = rows(c * 16 * w + x * 4 * w + z * w, w)
        local(t.at[3], dst.at[place], s4_l.at[i])
        for k in range(1, 4):
            send(t.at[3], dst.at[place], s4_s.at[i, k - 1], s4_r.at[i, k - 1], at.at_z((z + k) % 4))

    hidden(yl)
    hidden(yr)

    wait(hbuf.at[pl.ds(0, 3)], hy_r)
    horder = order_matrix(8, 4)
    hx = dot(horder, hbuf[...].reshape(256, 512)).astype(BF)
    hx = [hx[k * 32 : (k + 1) * 32] for k in range(8)]
    i0 = iota((128, 128), 0)
    j0 = iota((128, 128), 1)
    for odd in range(2):
        take_in = ones_where(jnp.logical_and(j0 < 64, i0 == j0 + 64 * odd))
        take_grad = ones_where(jnp.logical_and(j0 >= 64, i0 == j0 - 64 + 64 * odd))
        for b in range(16):
            q, o = b // 4, (b % 4) * 128
            block = dot(hx[q][:, o : o + 128], take_in) + dot(hx[4 + q][:, o : o + 128], take_grad)
            wsend[2 * b + odd] = block.astype(BF)
    local(wsend.at[at.e], wrecv.at[at.e], w_r)

    def widths(k, _):
        e = (at.e + k) % 32
        send(wsend.at[e], wrecv.at[at.e], w_s, w_r, (at.dp, e))
        return 0

    lax.fori_loop(1, 32, widths, 0)

    def half_of(dst, w):
        return lambda xx, b: dst.at[rows(c * 16 * w + xx * 4 * w + b * 2 * w, 2 * w)]

    def quarter_of(dst, w, xx):
        return dst.at[rows(c * 16 * w + xx * 4 * w, 4 * w)]

    for i, (dst, t, rr, w) in enumerate(full):
        wait(t.at[3], s4_l.at[i])
        for k in range(3):
            wait(t.at[3], s4_r.at[i, k])
        half = half_of(dst, w)
        for b in range(2):
            send(half(x, b), half(x, b), s5_s.at[i, b], s5_r.at[i, 0, b], at.at_x(xr))
            send(half(x, b), half(x, b), s5_s.at[i, 2 + b], s5_r.at[i, 1, b], at.at_x(xl))
        send(quarter_of(dst, w, x), quarter_of(dst, w, x), s6_s.at[i, 0], s6_r.at[i, 0], at.partner())

    for i in range(8):
        wait(slab(yo, groups[i]), y_f.at[i])
    hidden(yo)

    local_at = rows(at.e * 64, 64)

    def gradients(q):
        here = rows(q * 512, 512)
        gu[here] = dot_tn(xs[q], pre_s[...]).astype(BF)
        gd[here] = dot_tn(xs[4 + q], act_s[...]).astype(BF)

    def give_gradients(k, _, q):
        e = q * 8 + (at.e + k) % 8
        to = (at.dp, e)
        send(gu.at[rows(e * 64, 64)], ogu.at[at.e], g_s.at[0], g_r.at[0], to)
        send(gd.at[rows(e * 64, 64)], ogd.at[at.e], g_s.at[1], g_r.at[1], to)
        return 0

    def partial(s):
        at_s = rows(s * 128, 128)
        for q in range(4):
            cols = slice(q * 512, (q + 1) * 512)
            ys[q] = dot(act_s[at_s], dnv[:, cols]).astype(BF)
            ys[4 + q] = dot_nt(pre_s[at_s], upv[cols, :]).astype(BF)

        def unsort_rows(b, _):
            block = jnp.concatenate([ys[k, rows(b * 32, 32)] for k in range(8)], axis=0)
            parts[s, pl.ds(b * 16, 16)] = dot_tn(order, block).astype(BF).reshape(16, 16, 512)
            return 0

        lax.fori_loop(0, 4, unsort_rows, 0)

    def part(of_y, g):
        return parts.at[of_y, pl.ds(g * 8, 8)]

    for k in (2, 1):
        q = (z + k) % 4
        gradients(q)
        lax.fori_loop(0, 8, functools.partial(give_gradients, q=q), 0)
    partial(yo)
    for i in range(4):
        send(part(yo, i), m.at[0, i], m_s, m_r.at[0, i], at.at_y(yr))
        send(part(yo, 4 + i), m.at[1, i], m_s, m_r.at[1, i], at.at_y(yl))
    q = (z + 3) % 4
    gradients(q)
    lax.fori_loop(0, 8, functools.partial(give_gradients, q=q), 0)
    for s, to, first, side in ((yr, yr, 4, 0), (yl, yl, 0, 1)):
        partial(s)
        for i in range(4):
            send(part(s, first + i), r.at[side, first + i], raw_s, raw_r.at[side, i], at.at_y(to))
    gradients(z)
    local(gu.at[local_at], ogu.at[at.e], g_r.at[0])
    local(gd.at[local_at], ogd.at[at.e], g_r.at[1])
    lax.fori_loop(1, 8, functools.partial(give_gradients, q=z), 0)

    for i, (dst, t, rr, w) in enumerate(full):
        half = half_of(dst, w)
        wait(half(xl, 0), s5_r.at[i, 0, 0])
        send(half(xl, 0), half(xl, 0), s5_s.at[i, 4], s5_f.at[i, 0], at.at_x(xr))
        wait(half(xr, 1), s5_r.at[i, 1, 1])
        send(half(xr, 1), half(xr, 1), s5_s.at[i, 5], s5_f.at[i, 1], at.at_x(xl))

    for i in range(4):
        wait(m.at[0, i], m_r.at[0, i])
        m[0, i] = (m[0, i].astype(F32) + parts[yr, pl.ds(i * 8, 8)].astype(F32)).astype(BF)
        send(m.at[0, i], r.at[0, i], acc_s, acc_r.at[0, i], at.at_y(yr))
        wait(m.at[1, i], m_r.at[1, i])
        m[1, i] = (m[1, i].astype(F32) + parts[yl, pl.ds(32 + i * 8, 8)].astype(F32)).astype(BF)
        send(m.at[1, i], r.at[1, 4 + i], acc_s, acc_r.at[1, i], at.at_y(yl))
    partial(y)

    for i, (dst, t, rr, w) in enumerate(full):
        half = half_of(dst, w)
        wait(half(xl, 1), s5_r.at[i, 0, 1])
        wait(half(xr, 0), s5_r.at[i, 1, 0])
        for k, xx in ((1, xl), (2, xr)):
            send(quarter_of(dst, w, xx), quarter_of(dst, w, xx), s6_s.at[i, k], s6_r.at[i, k], at.partner())
    for i, (dst, t, rr, w) in enumerate(full):
        half = half_of(dst, w)
        wait(half(xo, 0), s5_f.at[i, 0])
        wait(half(xo, 1), s5_f.at[i, 1])
        send(quarter_of(dst, w, xo), quarter_of(dst, w, xo), s6_s.at[i, 3], s6_r.at[i, 3], at.partner())
    for i, (dst, t, rr, w) in enumerate(full):
        for k in range(4):
            wait(dst.at[pl.ds(0, 4 * w)], s6_r.at[i, k])

    preact = dot(hx[0], uph[0:512])
    dact = dot_nt(hx[4], dnh[:, 0:512])
    for q in range(1, 4):
        preact += dot(hx[q], uph[q * 512 : (q + 1) * 512])
        dact += dot_nt(hx[4 + q], dnh[:, q * 512 : (q + 1) * 512])
    value, slope = gelu_pair(preact)
    hact = value.astype(BF)
    hpre = (dact * slope).astype(BF)
    apack[:, 0:512] = hpre
    apack[:, 512:1024] = hact
    local(apack, apool.at[z, x, c], az_r.at[3])
    for k in range(1, 4):
        send(apack, apool.at[z, x, c], az_s, az_r.at[k - 1], at.at_z((z + k) % 4))
    outs = [dot(hact, dnh[:, q * 512 : (q + 1) * 512]).astype(BF) for q in range(4)]
    backs = [dot_nt(hpre, uph[q * 512 : (q + 1) * 512, :]).astype(BF) for q in range(4)]
    hout = dot_tn(horder, jnp.concatenate(outs + backs, axis=0)).astype(BF)
    hparts[...] = hout.reshape(4, 2, 32, 512)
    for k in range(1, 4):
        yy = (y + k) % 4
        send(hparts.at[yy], hr.at[k - 1], hp_s, hp_r.at[k - 1], at.at_y(yy))

    for i in range(8):
        side_raw, side_acc = (1, 0) if i < 4 else (0, 1)
        wait(r.at[side_raw, i], raw_r.at[side_raw, i % 4])
        wait(r.at[side_acc, i], acc_r.at[side_acc, i % 4])
        ret[pl.ds(i * 8, 8)] = (
            parts[y, pl.ds(i * 8, 8)].astype(F32) + r[0, i].astype(F32) + r[1, i].astype(F32)
        ).astype(BF)

        def give_back(j, _, i=i):
            p = i * 8 + j

            @pl.when(p != at.me)
            def _():
                send(ret.at[p], rbuf.at[at.me], ret_s, ret_r, at.at_peer(p))

            @pl.when(p == at.me)
            def _():
                local(ret.at[p], rbuf.at[p], ret_r)

            return 0

        lax.fori_loop(0, 8, give_back, 0)

    for k in range(4):
        wait(apack, az_r.at[k])
    for k in range(1, 4):
        send(apool.at[:, x, c], apool.at[:, x, c], ax_s, ax_r.at[k - 1], at.at_x((x + k) % 4))
    for k in range(3):
        wait(hr.at[k], hp_r.at[k])
    hret[...] = (
        hparts[y].astype(F32) + hr[0].astype(F32) + hr[1].astype(F32) + hr[2].astype(F32)
    ).astype(BF)
    local(hret.at[at.h], rhot.at[at.h], hret_r.at[0])
    send(hret.at[1 - at.h], rhot.at[at.h], hret_s, hret_r.at[1], at.at_peer((at.me + 32) % 64))
    for k in range(3):
        wait(apool.at[:, 0, 0], ax_r.at[k])
    send(apool.at[:, :, c], apool.at[:, :, c], ac_s, ac_r, at.partner())

    wait(wrecv, w_r)
    wait(apool.at[:, :, 0], ac_r)
    wide = wrecv[...].reshape(1024, 128)
    pool = apool[...].reshape(1024, 1024)
    hup_ref[...] = dot_tn(wide, pool[:, 0:512])[0:64].astype(BF)
    hdn_ref[...] = dot_tn(wide, pool[:, 512:1024])[64:128].astype(BF)

    wait(rbuf, ret_r)
    wait(rhot.at[0], hret_r.at[0])
    wait(rhot.at[0], hret_r.at[1])
    id_cols = [to_column(ids_ref[k : k + 1, :]) for k in range(2)]
    slot_cols = [to_column(slots_ref[k : k + 1, :]) for k in range(2)]
    combine_rows(hot, rbuf, rhot, gate_cols, id_cols, slot_cols, out_ref, back_ref)

    wait(ogu, g_r.at[0])
    wait(ogd, g_r.at[1])

    for i, (w, own, other, n) in enumerate(arrays):
        wait(own, s1_s.at[i])
    wait(buf.at[0, pl.ds(0, 63)], disp_s)
    wait(buf.at[pl.ds(0, 3)], y_s)
    wait(hbuf.at[pl.ds(0, 3)], hy_s)
    wait(hbuf.at[0, 0], h_s)
    for i, (o, mm, rr, t, n) in enumerate(ring):
        for k in range(6):
            wait(mm.at[0], s2_s.at[i, k])
        for k in range(3):
            wait(t.at[0], s3_s.at[i, k])
            wait(t.at[0], s4_s.at[i, k])
    for i, (dst, t, rr, w) in enumerate(full):
        for k in range(6):
            wait(dst.at[pl.ds(0, 2 * w)], s5_s.at[i, k])
        for k in range(4):
            wait(dst.at[pl.ds(0, 4 * w)], s6_s.at[i, k])
    wait(gu.at[pl.ds(0, 31 * 64)], g_s.at[0])
    wait(gd.at[pl.ds(0, 31 * 64)], g_s.at[1])
    wait(wsend.at[pl.ds(0, 31)], w_s)
    wait(m, m_s)
    wait(m, raw_s)
    wait(m, acc_s)
    wait(ret.at[pl.ds(0, 63)], ret_s)
    wait(hr, hp_s)
    wait(hret.at[0], hret_s)
    wait(apool.at[0, 0:3, 0], az_s)
    wait(apool.at[:, 0:3, 0], ax_s)
    wait(apool.at[:, :, 0], ac_s)


def layer(hot_mask, tokens, cotangent, gate_t, ids_t, slots_t, up, down):
    def vm(*shape):
        return pltpu.VMEM(shape, BF)

    return pl.pallas_call(
        layer_kernel,
        out_shape=(
            sds((128, 2048)), sds((128, 2048)), sds((64, 512)), sds((64, 512)),
            sds((32, 64, 512)), sds((32, 64, 512)),
        ),
        in_specs=[SM, VM, VM, VM, VM, VM, ANY, ANY],
        out_specs=(VM, VM, VM, VM, ANY, ANY),
        scratch_shapes=[
            vm(32, 16, 512), vm(32, 512), vm(4, 64, 16, 512), vm(4, 2, 32, 512),
            vm(2048, 512), vm(512, 2048), vm(2048, 512), vm(512, 2048),
            vm(1024, 512), vm(256, 2048), vm(1024, 512), vm(256, 2048),
            vm(2, 128, 512), vm(2, 32, 2048), vm(2, 256, 512), vm(2, 64, 2048),
            vm(4, 64, 512), vm(4, 16, 2048),
            vm(8, 512, 512), vm(512, 512), vm(512, 512), vm(8, 128, 512),
            vm(2048, 512), vm(2048, 512), vm(4, 64, 16, 512), vm(4, 2, 32, 512),
            vm(32, 1024), vm(32, 32, 128),
            vm(2, 4, 8, 16, 512), vm(2, 8, 8, 16, 512), vm(64, 16, 512), vm(64, 16, 512),
            vm(3, 2, 32, 512), vm(2, 32, 512), vm(2, 32, 512), vm(4, 4, 2, 32, 1024), vm(32, 32, 128),
            DMA((2,)), DMA, DMA((8,)), DMA, DMA((2, 8)), DMA((8,)), DMA, DMA((2,)), DMA, DMA,
            DMA((2,)), DMA((2,)), DMA((2,)),
            DMA((2, 6)), DMA((2, 2)), DMA((2, 2)), DMA((2, 2)),
            DMA((2, 3)), DMA((2, 3)), DMA((2, 3)), DMA((2, 3)), DMA((2,)),
            DMA((2, 6)), DMA((2, 2, 2)), DMA((2, 2)), DMA((2, 4)), DMA((2, 4)),
            DMA((2,)), DMA((2,)), DMA, DMA, DMA, DMA((2, 4)), DMA, DMA((2, 4)), DMA, DMA((2, 4)), DMA, DMA,
            DMA, DMA((3,)), DMA, DMA((2,)), DMA, DMA((4,)), DMA, DMA((3,)), DMA, DMA,
        ],
        compiler_params=pltpu.CompilerParams(
            collective_id=1, has_side_effects=True, vmem_limit_bytes=LIMIT
        ),
        name="layer",
    )(hot_mask, tokens, cotangent, gate_t, ids_t, slots_t, up, down)


def on_device(tokens, cotangent, gate_probs, expert_ids, route_slots, hot_mask, w_up, w_down):
    layer_out, grad_tokens, hup, hdn, ogu, ogd = layer(
        hot_mask, tokens, cotangent, gate_probs.T, expert_ids.T, route_slots.T, w_up[0], w_down[0]
    )
    is_hot = (hot_mask > 0)[:, None, None]
    grad_up = jnp.where(is_hot, hup[None], ogu)
    grad_down = jnp.where(is_hot, hdn[None], ogd)
    return (layer_out, grad_tokens, grad_up, grad_down)


def solution(mesh):
    placed = (
        P(("dp", "expert"), None),
        P(("dp", "expert"), None),
        P(("dp", "expert"), None),
        P(("dp", "expert"), None),
        P(("dp", "expert"), None),
        P(),
        P("expert", None, "dp"),
        P("expert", "dp", None),
    )
    return jax.shard_map(
        on_device,
        mesh=mesh,
        in_specs=placed,
        out_specs=(
            P(("dp", "expert"), None),
            P(("dp", "expert"), None),
            P(None, "expert", "dp"),
            P(None, "expert", "dp"),
        ),
        check_vma=False,
    )
```

```python
import functools

import jax
import jax.numpy as jnp
from jax import lax
from jax.experimental import pallas as pl
from jax.experimental.pallas import tpu as pltpu
from jax.sharding import PartitionSpec as P

CAP = 2
HCAP = 4
MESH = pl.DeviceIdType.MESH
BF = jnp.bfloat16
F32 = jnp.float32
ANY = pl.BlockSpec(memory_space=pl.ANY)
VM = pl.BlockSpec(memory_space=pltpu.VMEM)
SM = pl.BlockSpec(memory_space=pltpu.SMEM)
DMA = pltpu.SemaphoreType.DMA
Z_OFFSETS = (0, 1, 7, 2, 6, 3, 5, 4)
LIMIT = 60 * 1024 * 1024


def sds(shape, dtype=BF):
    return jax.ShapeDtypeStruct(shape, dtype)


def iota(shape, dim):
    return lax.broadcasted_iota(jnp.int32, shape, dim)


def dot(a, b):
    return jnp.dot(a, b, preferred_element_type=F32)


def dot_nt(a, b):
    return lax.dot_general(a, b, (((1,), (1,)), ((), ())), preferred_element_type=F32)


def dot_tn(a, b):
    return lax.dot_general(a, b, (((0,), (0,)), ((), ())), preferred_element_type=F32)


def ones_where(cond):
    return jnp.where(cond, 1.0, 0.0).astype(BF)


class Place:
    def __init__(self):
        self.dp = lax.axis_index("dp")
        self.e = lax.axis_index("expert")
        self.h = self.dp // 4
        self.y = self.dp % 4
        self.z = self.e // 8
        self.x = (self.e // 2) % 4
        self.c = self.e % 2
        self.me = self.h * 32 + self.e
        self.group = self.me // 8

    def at_y(self, y):
        return (self.h * 4 + y, self.e)

    def at_x(self, x):
        return (self.dp, self.z * 8 + x * 2 + self.c)

    def at_z(self, z):
        return (self.dp, z * 8 + self.x * 2 + self.c)

    def partner(self):
        return (self.dp, self.e + 1 - 2 * self.c)

    def at_peer(self, p):
        return ((p // 32) * 4 + self.y, p % 32)


def send(src, dst, ssem, rsem, to):
    copy = pltpu.make_async_remote_copy(
        src_ref=src, dst_ref=dst, send_sem=ssem, recv_sem=rsem, device_id=to, device_id_type=MESH
    )
    copy.start()


def local(src, dst, sem):
    pltpu.make_async_copy(src, dst, sem).start()


def wait(ref, sem):
    pltpu.make_async_copy(ref, ref, sem).wait()


def rows(start, size):
    return pl.ds(pl.multiple_of(start, 16), size)


def gelu_pair(preact):
    normal_cdf = 0.5 * (1.0 + lax.erf(preact * 0.7071067811865476))
    density = jnp.exp(-0.5 * preact * preact) * 0.3989422804014327
    return (preact * normal_cdf, normal_cdf + preact * density)


def order_matrix(src_count, slot_count):
    r = iota((256, 256), 0)
    k = iota((256, 256), 1)
    slot = r % slot_count
    src = (r // slot_count) % src_count
    q = (r // 32) % 4
    a = r // 128
    return ones_where(k == src * (8 * slot_count) + a * (4 * slot_count) + slot * 4 + q)


def to_column(row):
    wide = row.shape[1]
    same = iota((wide, wide), 0) == iota((wide, wide), 1)
    return jnp.sum(jnp.where(same, row, jnp.zeros_like(row)), axis=1, keepdims=True)


def places_of(ids, slot, hot):
    is_hot = ids == hot
    normal = jnp.where(jnp.logical_and(jnp.logical_not(is_hot), slot < CAP), ids * CAP + slot, -1)
    special = jnp.where(jnp.logical_and(is_hot, slot < HCAP), slot, -1)
    return normal, special


def pack_rows(hot, tokens, cot, gate_cols, ids, slots, disp, hrow):
    r = iota((512, 128), 0)
    code = (r // 16) * CAP + (r // 4) % 2
    is_grad = (r // 8) % 2
    quarter = r % 4
    hr = iota((32, 128), 0)
    hcode = (hr // 4) % 4
    h_is_grad = hr // 16
    hquarter = hr % 4
    sel, hsel = [], []
    for k in range(2):
        normal, special = places_of(ids[k : k + 1, :], slots[k : k + 1, :], hot)
        sel.append(code == normal)
        hsel.append(hcode == special)
    either = jnp.logical_or(sel[0], sel[1])
    heither = jnp.logical_or(hsel[0], hsel[1])
    out = jnp.zeros((512, 512), F32)
    hout = jnp.zeros((32, 512), F32)
    for q in range(4):
        cols = slice(q * 512, (q + 1) * 512)
        wide = cot[:, cols].astype(F32)
        parts = (
            (tokens[:, cols], either, heither, 0),
            ((gate_cols[0] * wide).astype(BF), sel[0], hsel[0], 1),
            ((gate_cols[1] * wide).astype(BF), sel[1], hsel[1], 1),
        )
        for data, s, hs, kind in parts:
            m = ones_where(jnp.logical_and(jnp.logical_and(s, quarter == q), is_grad == kind))
            out += dot(m, data)
            hm = ones_where(jnp.logical_and(jnp.logical_and(hs, hquarter == q), h_is_grad == kind))
            hout += dot(hm, data)
    disp[...] = out.astype(BF).reshape(32, 16, 512)
    hrow[...] = hout.astype(BF)


def pack_columns(hot, tokens, cot, gate_cols, ids, slots, edisp):
    r = iota((512, 128), 0)
    dest = r // 16
    z = dest // 8
    code = ((2 - z // 2) * 8 + dest % 8) * CAP + (r // 4) % 2
    is_grad = (r // 8) % 2
    piece = z * 4 + r % 4
    sel = [code == places_of(ids[k : k + 1, :], slots[k : k + 1, :], hot)[0] for k in range(2)]
    either = jnp.logical_or(sel[0], sel[1])
    masks = [
        jnp.logical_and(s, is_grad == kind) for s, kind in ((either, 0), (sel[0], 1), (sel[1], 1))
    ]
    for q in range(4):
        here = slice(q * 128, (q + 1) * 128)
        out = jnp.zeros((128, 128), F32)
        for p in range(4 * q, 4 * q + 4):
            cols = slice(p * 128, (p + 1) * 128)
            wide = cot[:, cols].astype(F32)
            data = (tokens[:, cols], (gate_cols[0] * wide).astype(BF), (gate_cols[1] * wide).astype(BF))
            for d, mask in zip(data, masks):
                out += dot(ones_where(jnp.logical_and(mask, piece == p)[here]), d)
        edisp[q * 8 : (q + 1) * 8] = out.astype(BF).reshape(8, 16, 128)


def combine_rows(hot, rbuf, rhot, gate_cols, id_cols, slot_cols, out_ref, back_ref):
    r = iota((128, 1024), 1)
    code = ((r // 16) % 32) * CAP + (r // 4) % 2
    is_back = (r // 8) % 2
    quarter = r % 4
    hr = iota((128, 64), 1)
    hcode = (hr // 4) % 4
    h_is_back = (hr // 16) % 2
    hquarter = hr % 4
    sel, hsel = [], []
    for k in range(2):
        normal, special = places_of(id_cols[k], slot_cols[k], hot)
        sel.append(code == normal)
        hsel.append(hcode == special)
    data = rbuf[...].reshape(1024, 512)
    hdata = rhot[...].reshape(64, 512)

    def pick(s, hs, q, kind):
        m = ones_where(jnp.logical_and(jnp.logical_and(s, quarter == q), is_back == kind))
        hm = ones_where(jnp.logical_and(jnp.logical_and(hs, hquarter == q), h_is_back == kind))
        return dot(m, data) + dot(hm, hdata)

    either = jnp.logical_or(sel[0], sel[1])
    heither = jnp.logical_or(hsel[0], hsel[1])
    for q in range(4):
        cols = slice(q * 512, (q + 1) * 512)
        out = gate_cols[0] * pick(sel[0], hsel[0], q, 0) + gate_cols[1] * pick(sel[1], hsel[1], q, 0)
        out_ref[:, cols] = out.astype(BF)
        back_ref[:, cols] = pick(either, heither, q, 1).astype(BF)


def layer_kernel(
    mask_ref, tokens, cot, gate_ref, ids_ref, slots_ref, up, down,
    out_ref, back_ref, hup_ref, hdn_ref, ogu, ogd,
    disp, hrow, buf, hbuf, upv, dnv, uph, dnh,
    p_up, p_dn, o_up, o_dn, m_up, m_dn, r_up, r_dn, t_up, t_dn,
    edisp, ebuf, xe, pa, epa, egu, egd,
    xs, ys, gu, gd, parts, hparts, apack, wsend,
    m, r, ret, rbuf, hr, hret, rhot, apool, wrecv,
    load_s, disp_s, disp_r, y_s, y_r, y_f, h_s, h_r, hy_s, hy_r,
    s1_s, s1_r, s1_l, s2_s, s2_m, s2_raw, s2_acc, s3_s, s3_r, s5_s, s5_r, s5_f, s6_s, s6_r,
    g_s, g_r, w_s, w_r, m_s, m_r, raw_s, raw_r, acc_s, acc_r, ret_s, ret_r,
    hp_s, hp_r, hret_s, hret_r, az_s, az_r, ax_s, ax_r, ac_s, ac_r,
    ed_s, ed_r, ey_s, ey_r, ey_f, em_s, em_r, ef_s, eg_s,
):
    at = Place()
    y, x, z, c = at.y, at.x, at.z, at.c
    yr, yl, yo = (y + 1) % 4, (y + 3) % 4, (y + 2) % 4
    xr, xl, xo = (x + 1) % 4, (x + 3) % 4, (x + 2) % 4

    barrier = pltpu.get_barrier_semaphore()

    def greet(k, _):
        pl.semaphore_signal(barrier, inc=1, device_id=at.at_peer((at.me + k) % 64), device_id_type=MESH)
        return 0

    lax.fori_loop(1, 64, greet, 0)
    for k in range(1, 4):
        pl.semaphore_signal(barrier, inc=1, device_id=at.at_y((y + k) % 4), device_id_type=MESH)

    arrays = ((up, o_up, p_up, 1024), (down, o_dn, p_dn, 256))
    for i, (w, own, _, n) in enumerate(arrays):
        local(w.at[rows(c * n, n)], own, s1_l.at[i])
    local(up, upv, load_s.at[0])
    local(down, dnv, load_s.at[1])

    hot = mask_ref[0] * 0
    for k in range(1, 32):
        hot += mask_ref[k] * k
    f_own = jnp.where(hot == at.e, 1.0, 0.0)
    f_other = jnp.where(hot == at.e + 1 - 2 * c, 1.0, 0.0)
    gate_cols = [to_column(gate_ref[k : k + 1, :]) for k in range(2)]
    pack_rows(hot, tokens, cot, gate_cols, ids_ref, slots_ref, disp, hrow)

    pl.semaphore_wait(barrier, 66)

    for i, (w, _, other, n) in enumerate(arrays):
        send(w.at[rows((1 - c) * n, n)], other, s1_s.at[i], s1_r.at[i], at.partner())

    local(disp.at[at.e], buf.at[y, at.me], disp_r.at[at.group])
    groups = [(at.group + off) % 8 for off in Z_OFFSETS]
    for i, off in enumerate(Z_OFFSETS):

        def dispatch(k, _, g=groups[i]):
            p = g * 8 + (at.me + k) % 8
            send(disp.at[p % 32], buf.at[y, at.me], disp_s, disp_r.at[at.group], at.at_peer(p))
            return 0

        lax.fori_loop(1 if i == 0 else 0, 8, dispatch, 0)
    local(hrow, hbuf.at[y, at.h], h_r.at[0])
    send(hrow, hbuf.at[y, at.h], h_s, h_r.at[1], at.at_peer((at.me + 32) % 64))

    for i, (w, own, other, n) in enumerate(arrays):
        wait(own, s1_l.at[i])
        wait(other, s1_r.at[i])
    for own, other, n in ((o_up, p_up, 1024), (o_dn, p_dn, 256)):

        def choose(k, _, own=own, other=other, n=n):
            s = rows(k * (n // 16), n // 16)
            own[s] = (own[s].astype(F32) * f_own + other[s].astype(F32) * f_other).astype(BF)
            return 0

        lax.fori_loop(0, 16, choose, 0)

    ring = ((o_up, m_up, r_up, t_up, 128), (o_dn, m_dn, r_dn, t_dn, 32))
    full = ((uph, t_up, r_up, 64), (dnh, t_dn, r_dn, 16))

    def hot_begin(i):
        o, mm, rr, t, n = ring[i]
        send(o.at[rows(xo * 2 * n, n)], mm.at[0], s2_s.at[i, 0], s2_m.at[i, 0], at.at_x(xr))
        send(o.at[rows(xo * 2 * n + n, n)], mm.at[1], s2_s.at[i, 1], s2_m.at[i, 1], at.at_x(xl))
        send(o.at[rows(xr * 2 * n + n, n)], rr.at[0, pl.ds(n, n)], s2_s.at[i, 2], s2_raw.at[i, 0], at.at_x(xr))
        send(o.at[rows(xl * 2 * n, n)], rr.at[1, pl.ds(0, n)], s2_s.at[i, 3], s2_raw.at[i, 1], at.at_x(xl))

    def hot_ring(i):
        o, mm, rr, t, n = ring[i]
        wait(mm.at[0], s2_m.at[i, 0])
        mm[0] = mm[0] + o[rows(xr * 2 * n, n)]
        send(mm.at[0], rr.at[0, pl.ds(0, n)], s2_s.at[i, 4], s2_acc.at[i, 0], at.at_x(xr))
        wait(mm.at[1], s2_m.at[i, 1])
        mm[1] = mm[1] + o[rows(xl * 2 * n + n, n)]
        send(mm.at[1], rr.at[1, pl.ds(n, n)], s2_s.at[i, 5], s2_acc.at[i, 1], at.at_x(xl))

    def hot_line(i):
        o, mm, rr, t, n = ring[i]
        for side, raw, acc in ((0, pl.ds(n, n), pl.ds(0, n)), (1, pl.ds(0, n), pl.ds(n, n))):
            wait(rr.at[side, raw], s2_raw.at[i, side])
            wait(rr.at[side, acc], s2_acc.at[i, side])
        rr[0] = rr[0] + rr[1] + o[rows(x * 2 * n, 2 * n)]

        @pl.when(z == 0)
        def _():
            send(rr.at[0], t.at[0], s3_s.at[i, 0], s3_r.at[i, 0], at.at_z(1))

        @pl.when(z == 3)
        def _():
            send(rr.at[0], t.at[1], s3_s.at[i, 1], s3_r.at[i, 1], at.at_z(2))

    def hot_up(i):
        o, mm, rr, t, n = ring[i]

        @pl.when(z > 0)
        def _():
            wait(t.at[0], s3_r.at[i, 0])

            @pl.when(z < 3)
            def _():
                t[2] = t[0] + rr[0]
                send(t.at[2], t.at[0], s3_s.at[i, 0], s3_r.at[i, 0], at.at_z(z + 1))

    def hot_down(i):
        o, mm, rr, t, n = ring[i]

        @pl.when(z < 3)
        def _():
            wait(t.at[1], s3_r.at[i, 1])

            @pl.when(z > 0)
            def _():
                t[3] = t[1] + rr[0]
                send(t.at[3], t.at[1], s3_s.at[i, 1], s3_r.at[i, 1], at.at_z(z - 1))

    def hot_near():
        @pl.when(z < 2)
        def _():
            hot_up(0)
            hot_up(1)

        @pl.when(z >= 2)
        def _():
            hot_down(0)
            hot_down(1)

    def hot_far():
        @pl.when(z < 2)
        def _():
            hot_down(0)
            hot_down(1)

        @pl.when(z >= 2)
        def _():
            hot_up(0)
            hot_up(1)

    def half_of(dst, w):
        return lambda xx, b: dst.at[rows(c * 16 * w + xx * 4 * w + b * 2 * w, 2 * w)]

    def quarter_of(dst, w, xx):
        return dst.at[rows(c * 16 * w + xx * 4 * w, 4 * w)]

    def hot_around(i):
        dst, t, rr, w = full[i]
        mine = rows(c * 16 * w + x * 4 * w, 4 * w)

        @pl.when(z == 0)
        def _():
            dst[mine] = rr[0] + t[1]

        @pl.when(z == 3)
        def _():
            dst[mine] = rr[0] + t[0]

        @pl.when(jnp.logical_and(z > 0, z < 3))
        def _():
            dst[mine] = rr[0] + t[0] + t[1]

        half = half_of(dst, w)
        for b in range(2):
            send(half(x, b), half(x, b), s5_s.at[i, b], s5_r.at[i, 0, b], at.at_x(xr))
            send(half(x, 1 - b), half(x, 1 - b), s5_s.at[i, 2 + b], s5_r.at[i, 1, 1 - b], at.at_x(xl))
        send(quarter_of(dst, w, x), quarter_of(dst, w, x), s6_s.at[i, 0], s6_r.at[i, 0], at.partner())

    def hot_onward(i):
        dst, t, rr, w = full[i]
        half = half_of(dst, w)
        wait(half(xl, 0), s5_r.at[i, 0, 0])
        send(half(xl, 0), half(xl, 0), s5_s.at[i, 4], s5_f.at[i, 0], at.at_x(xr))
        wait(half(xr, 1), s5_r.at[i, 1, 1])
        send(half(xr, 1), half(xr, 1), s5_s.at[i, 5], s5_f.at[i, 1], at.at_x(xl))

    def hot_partner(i):
        dst, t, rr, w = full[i]
        half = half_of(dst, w)
        wait(half(xl, 1), s5_r.at[i, 0, 1])
        wait(half(xr, 0), s5_r.at[i, 1, 0])
        for k, xx in ((1, xl), (2, xr)):
            send(quarter_of(dst, w, xx), quarter_of(dst, w, xx), s6_s.at[i, k], s6_r.at[i, k], at.partner())

    def hot_last(i):
        dst, t, rr, w = full[i]
        half = half_of(dst, w)
        wait(half(xo, 0), s5_f.at[i, 0])
        wait(half(xo, 1), s5_f.at[i, 1])
        send(quarter_of(dst, w, xo), quarter_of(dst, w, xo), s6_s.at[i, 3], s6_r.at[i, 3], at.partner())

    def hot_arrived():
        for i, (dst, t, rr, w) in enumerate(full):
            for k in range(4):
                wait(dst.at[pl.ds(0, 4 * w)], s6_r.at[i, k])

    for i in range(2):
        hot_begin(i)

    def slab(of_y, g):
        return buf.at[of_y, pl.ds(g * 8, 8)]

    def pass_on(i):
        g = groups[i]
        wait(slab(y, g), disp_r.at[g])
        send(slab(y, g), slab(y, g), y_s, y_r.at[0, i], at.at_y(yr))
        send(slab(y, g), slab(y, g), y_s, y_r.at[1, i], at.at_y(yl))

    def forward(i):
        g = groups[i]
        wait(slab(yl, g), y_r.at[0, i])
        if i % 2 == 0:
            send(slab(yl, g), slab(yl, g), y_s, y_f.at[i], at.at_y(yr))
        wait(slab(yr, g), y_r.at[1, i])
        if i % 2 == 1:
            send(slab(yr, g), slab(yr, g), y_s, y_f.at[i], at.at_y(yl))

    order = order_matrix(16, 2)

    def hidden(s):
        def sort_rows(b, _):
            data = buf[s, pl.ds(b * 16, 16)].reshape(256, 512)
            block = dot(order, data).astype(BF)
            for k in range(8):
                xs[k, rows(s * 128 + b * 32, 32)] = block[k * 32 : (k + 1) * 32]
            return 0

        lax.fori_loop(0, 4, sort_rows, 0)
        at_s = rows(s * 128, 128)
        preact = dot(xs[0, at_s], upv[0:512])
        dact = dot_nt(xs[4, at_s], dnv[:, 0:512])
        for q in range(1, 4):
            preact += dot(xs[q, at_s], upv[q * 512 : (q + 1) * 512])
            dact += dot_nt(xs[4 + q, at_s], dnv[:, q * 512 : (q + 1) * 512])
        value, slope = gelu_pair(preact)
        pa[1, at_s] = value.astype(BF)
        pa[0, at_s] = (dact * slope).astype(BF)

    inner = jnp.logical_or(z == 1, z == 2)

    def share(i, s):
        at_s = rows(s * 128, 128)

        @pl.when(inner)
        def _():
            send(pa.at[:, at_s], epa.at[:, at_s], em_s, em_r.at[i], at.at_z(3 - z))

    def share_outward(i, s):
        at_s = rows(s * 128, 128)
        wait(epa.at[:, at_s], em_r.at[i])

        @pl.when(inner)
        def _():
            send(epa.at[:, at_s], epa.at[:, at_s], ef_s, em_r.at[i], at.at_z(3 * (z - 1)))

    for i in range(5):
        pass_on(i)
    hot_ring(0)
    hot_ring(1)
    for i in range(5, 8):
        pass_on(i)

    wait(hbuf.at[y, at.h], h_r.at[0])
    wait(hbuf.at[y, 1 - at.h], h_r.at[1])
    for k in range(1, 4):
        send(hbuf.at[y], hbuf.at[y], hy_s, hy_r, at.at_y((y + k) % 4))

    forward(0)
    forward(1)
    pack_columns(hot, tokens, cot, gate_cols, ids_ref, slots_ref, edisp)
    local(edisp.at[at.e], ebuf.at[y, at.me], ed_r)

    def dispatch_columns(k, _):
        p = (at.me + k) % 64
        send(edisp.at[p % 32], ebuf.at[y, at.me], ed_s, ed_r, at.at_peer(p))
        return 0

    lax.fori_loop(1, 64, dispatch_columns, 0)
    forward(2)
    forward(3)
    wait(upv, load_s.at[0])
    wait(dnv, load_s.at[1])
    hidden(y)
    share(0, y)
    hot_line(0)
    hot_line(1)
    for i in range(4, 8):
        forward(i)
    hot_near()
    hidden(yl)
    share(1, yl)
    wait(ebuf.at[y], ed_r)
    send(ebuf.at[y], ebuf.at[y], ey_s, ey_r.at[0], at.at_y(yr))
    send(ebuf.at[y], ebuf.at[y], ey_s, ey_r.at[1], at.at_y(yl))
    share_outward(0, y)
    hidden(yr)
    share(2, yr)
    hot_far()

    wait(hbuf.at[pl.ds(0, 3)], hy_r)
    horder = order_matrix(8, 4)
    hx = dot(horder, hbuf[...].reshape(256, 512)).astype(BF)
    hx = [hx[k * 32 : (k + 1) * 32] for k in range(8)]
    i0 = iota((128, 128), 0)
    j0 = iota((128, 128), 1)
    for odd in range(2):
        take_in = ones_where(jnp.logical_and(j0 < 64, i0 == j0 + 64 * odd))
        take_grad = ones_where(jnp.logical_and(j0 >= 64, i0 == j0 - 64 + 64 * odd))
        for b in range(16):
            q, o = b // 4, (b % 4) * 128
            block = dot(hx[q][:, o : o + 128], take_in) + dot(hx[4 + q][:, o : o + 128], take_grad)
            wsend[2 * b + odd] = block.astype(BF)
    local(wsend.at[at.e], wrecv.at[at.e], w_r)

    def widths(k, _):
        e = (at.e + k) % 32
        send(wsend.at[e], wrecv.at[at.e], w_s, w_r, (at.dp, e))
        return 0

    lax.fori_loop(1, 32, widths, 0)

    hot_around(0)
    hot_around(1)
    share_outward(1, yl)
    for i in range(8):
        wait(slab(yo, groups[i]), y_f.at[i])
    hidden(yo)
    share(3, yo)
    share_outward(2, yr)

    local_at = rows(at.e * 64, 64)

    def gradients(q):
        here = rows(q * 512, 512)
        gu[here] = dot_tn(xs[q], pa[0]).astype(BF)
        gd[here] = dot_tn(xs[4 + q], pa[1]).astype(BF)

    def give_gradients(k, _, q):
        e = q * 8 + (at.e + k) % 8
        to = (at.dp, e)
        send(gu.at[rows(e * 64, 64)], ogu.at[at.e], g_s.at[0], g_r.at[0], to)
        send(gd.at[rows(e * 64, 64)], ogd.at[at.e], g_s.at[1], g_r.at[1], to)
        return 0

    def partial(s):
        at_s = rows(s * 128, 128)
        for q in range(4):
            cols = slice(q * 512, (q + 1) * 512)
            ys[q] = dot(pa[1, at_s], dnv[:, cols]).astype(BF)
            ys[4 + q] = dot_nt(pa[0, at_s], upv[cols, :]).astype(BF)

        def unsort_rows(b, _):
            block = jnp.concatenate([ys[k, rows(b * 32, 32)] for k in range(8)], axis=0)
            parts[s, pl.ds(b * 16, 16)] = dot_tn(order, block).astype(BF).reshape(16, 16, 512)
            return 0

        lax.fori_loop(0, 4, unsort_rows, 0)

    def part(of_y, g):
        return parts.at[of_y, pl.ds(g * 8, 8)]

    def direct(k):
        q = (z + k) % 4
        crosses = (z // 2) != (q // 2)

        @pl.when(jnp.logical_not(jnp.logical_and(inner, crosses)))
        def _():
            gradients(q)
            lax.fori_loop(0, 8, functools.partial(give_gradients, q=q), 0)

    direct(2)
    direct(1)
    share_outward(3, yo)
    partial(yo)
    for i in range(4):
        send(part(yo, i), m.at[0, i], m_s, m_r.at[0, i], at.at_y(yr))
        send(part(yo, 4 + i), m.at[1, i], m_s, m_r.at[1, i], at.at_y(yl))
    wait(ebuf.at[yl], ey_r.at[0])
    send(ebuf.at[yl, pl.ds(0, 32)], ebuf.at[yl, pl.ds(0, 32)], ey_s, ey_f.at[0], at.at_y(yr))
    wait(ebuf.at[yr], ey_r.at[1])
    send(ebuf.at[yr, pl.ds(32, 32)], ebuf.at[yr, pl.ds(32, 32)], ey_s, ey_f.at[1], at.at_y(yl))
    direct(3)
    for s, to, first, side in ((yr, yr, 4, 0), (yl, yl, 0, 1)):
        partial(s)
        for i in range(4):
            send(part(s, first + i), r.at[side, first + i], raw_s, raw_r.at[side, i], at.at_y(to))
    gradients(z)
    local(gu.at[local_at], ogu.at[at.e], g_r.at[0])
    local(gd.at[local_at], ogd.at[at.e], g_r.at[1])
    lax.fori_loop(1, 8, functools.partial(give_gradients, q=z), 0)

    hot_onward(0)
    hot_onward(1)

    for i in range(4):
        wait(m.at[0, i], m_r.at[0, i])
        m[0, i] = (m[0, i].astype(F32) + parts[yr, pl.ds(i * 8, 8)].astype(F32)).astype(BF)
        send(m.at[0, i], r.at[0, i], acc_s, acc_r.at[0, i], at.at_y(yr))
        wait(m.at[1, i], m_r.at[1, i])
        m[1, i] = (m[1, i].astype(F32) + parts[yl, pl.ds(32 + i * 8, 8)].astype(F32)).astype(BF)
        send(m.at[1, i], r.at[1, 4 + i], acc_s, acc_r.at[1, i], at.at_y(yl))
    wait(ebuf.at[yo, pl.ds(0, 32)], ey_f.at[0])
    wait(ebuf.at[yo, pl.ds(32, 32)], ey_f.at[1])

    def sort_columns(b, _):
        s = b // 4
        data = ebuf[s, pl.ds((b % 4) * 16, 16)].reshape(256, 128)
        block = dot(order, data).astype(BF)
        for k in range(8):
            xe[k // 4, rows(b * 32, 32), (k % 4) * 128 : (k % 4 + 1) * 128] = block[k * 32 : (k + 1) * 32]
        return 0

    lax.fori_loop(0, 16, sort_columns, 0)
    egu[...] = dot_tn(xe[0], epa[0]).astype(BF)
    egd[...] = dot_tn(xe[1], epa[1]).astype(BF)
    other_expert = (2 - z // 2) * 8 + at.e % 8
    local(egu.at[rows((at.e % 8) * 64, 64)], ogu.at[other_expert], g_r.at[0])
    local(egd.at[rows((at.e % 8) * 64, 64)], ogd.at[other_expert], g_r.at[1])

    def give_other(k, _):
        j = (at.e + k) % 8
        to = (at.dp, z * 8 + j)
        send(egu.at[rows(j * 64, 64)], ogu.at[other_expert], eg_s.at[0], g_r.at[0], to)
        send(egd.at[rows(j * 64, 64)], ogd.at[other_expert], eg_s.at[1], g_r.at[1], to)
        return 0

    lax.fori_loop(1, 8, give_other, 0)
    partial(y)

    hot_partner(0)
    hot_partner(1)
    hot_last(0)
    hot_last(1)

    hot_arrived()

    preact = dot(hx[0], uph[0:512])
    dact = dot_nt(hx[4], dnh[:, 0:512])
    for q in range(1, 4):
        preact += dot(hx[q], uph[q * 512 : (q + 1) * 512])
        dact += dot_nt(hx[4 + q], dnh[:, q * 512 : (q + 1) * 512])
    value, slope = gelu_pair(preact)
    hact = value.astype(BF)
    hpre = (dact * slope).astype(BF)
    apack[:, 0:512] = hpre
    apack[:, 512:1024] = hact
    local(apack, apool.at[z, x, c], az_r.at[3])
    for k in range(1, 4):
        send(apack, apool.at[z, x, c], az_s, az_r.at[k - 1], at.at_z((z + k) % 4))
    outs = [dot(hact, dnh[:, q * 512 : (q + 1) * 512]).astype(BF) for q in range(4)]
    backs = [dot_nt(hpre, uph[q * 512 : (q + 1) * 512, :]).astype(BF) for q in range(4)]
    hout = dot_tn(horder, jnp.concatenate(outs + backs, axis=0)).astype(BF)
    hparts[...] = hout.reshape(4, 2, 32, 512)
    for k in range(1, 4):
        yy = (y + k) % 4
        send(hparts.at[yy], hr.at[k - 1], hp_s, hp_r.at[k - 1], at.at_y(yy))

    for i in range(8):
        side_raw, side_acc = (1, 0) if i < 4 else (0, 1)
        wait(r.at[side_raw, i], raw_r.at[side_raw, i % 4])
        wait(r.at[side_acc, i], acc_r.at[side_acc, i % 4])
        ret[pl.ds(i * 8, 8)] = (
            parts[y, pl.ds(i * 8, 8)].astype(F32) + r[0, i].astype(F32) + r[1, i].astype(F32)
        ).astype(BF)

        def give_back(j, _, i=i):
            p = i * 8 + j

            @pl.when(p != at.me)
            def _():
                send(ret.at[p], rbuf.at[at.me], ret_s, ret_r, at.at_peer(p))

            @pl.when(p == at.me)
            def _():
                local(ret.at[p], rbuf.at[p], ret_r)

            return 0

        lax.fori_loop(0, 8, give_back, 0)

    for k in range(4):
        wait(apack, az_r.at[k])
    for k in range(1, 4):
        send(apool.at[:, x, c], apool.at[:, x, c], ax_s, ax_r.at[k - 1], at.at_x((x + k) % 4))
    for k in range(3):
        wait(hr.at[k], hp_r.at[k])
    hret[...] = (
        hparts[y].astype(F32) + hr[0].astype(F32) + hr[1].astype(F32) + hr[2].astype(F32)
    ).astype(BF)
    local(hret.at[at.h], rhot.at[at.h], hret_r.at[0])
    send(hret.at[1 - at.h], rhot.at[at.h], hret_s, hret_r.at[1], at.at_peer((at.me + 32) % 64))
    for k in range(3):
        wait(apool.at[:, 0, 0], ax_r.at[k])
    send(apool.at[:, :, c], apool.at[:, :, c], ac_s, ac_r, at.partner())

    wait(wrecv, w_r)
    wait(apool.at[:, :, 0], ac_r)
    wide = wrecv[...].reshape(1024, 128)
    pool = apool[...].reshape(1024, 1024)
    hup_ref[...] = dot_tn(wide, pool[:, 0:512])[0:64].astype(BF)
    hdn_ref[...] = dot_tn(wide, pool[:, 512:1024])[64:128].astype(BF)

    wait(rbuf, ret_r)
    wait(rhot.at[0], hret_r.at[0])
    wait(rhot.at[0], hret_r.at[1])
    id_cols = [to_column(ids_ref[k : k + 1, :]) for k in range(2)]
    slot_cols = [to_column(slots_ref[k : k + 1, :]) for k in range(2)]
    combine_rows(hot, rbuf, rhot, gate_cols, id_cols, slot_cols, out_ref, back_ref)

    wait(ogu, g_r.at[0])
    wait(ogd, g_r.at[1])

    for i, (w, own, other, n) in enumerate(arrays):
        wait(own, s1_s.at[i])
    wait(buf.at[0, pl.ds(0, 63)], disp_s)
    wait(buf.at[pl.ds(0, 3)], y_s)
    wait(hbuf.at[pl.ds(0, 3)], hy_s)
    wait(hbuf.at[0, 0], h_s)
    for i, (o, mm, rr, t, n) in enumerate(ring):
        for k in range(6):
            wait(mm.at[0], s2_s.at[i, k])

        @pl.when(z < 3)
        def _(i=i, t=t):
            wait(t.at[0], s3_s.at[i, 0])

        @pl.when(z > 0)
        def _(i=i, t=t):
            wait(t.at[0], s3_s.at[i, 1])

    for i, (dst, t, rr, w) in enumerate(full):
        for k in range(6):
            wait(dst.at[pl.ds(0, 2 * w)], s5_s.at[i, k])
        for k in range(4):
            wait(dst.at[pl.ds(0, 4 * w)], s6_s.at[i, k])
    @pl.when(jnp.logical_not(inner))
    def _():
        wait(gu.at[pl.ds(0, 31 * 64)], g_s.at[0])
        wait(gd.at[pl.ds(0, 31 * 64)], g_s.at[1])

    @pl.when(inner)
    def _():
        wait(gu.at[pl.ds(0, 15 * 64)], g_s.at[0])
        wait(gd.at[pl.ds(0, 15 * 64)], g_s.at[1])
        wait(epa, em_s)
        wait(epa, ef_s)

    wait(egu.at[pl.ds(0, 7 * 64)], eg_s.at[0])
    wait(egd.at[pl.ds(0, 7 * 64)], eg_s.at[1])
    wait(ebuf.at[0, pl.ds(0, 63)], ed_s)
    wait(ebuf.at[pl.ds(0, 3)], ey_s)
    wait(wsend.at[pl.ds(0, 31)], w_s)
    wait(m, m_s)
    wait(m, raw_s)
    wait(m, acc_s)
    wait(ret.at[pl.ds(0, 63)], ret_s)
    wait(hr, hp_s)
    wait(hret.at[0], hret_s)
    wait(apool.at[0, 0:3, 0], az_s)
    wait(apool.at[:, 0:3, 0], ax_s)
    wait(apool.at[:, :, 0], ac_s)


def layer(hot_mask, tokens, cotangent, gate_t, ids_t, slots_t, up, down):
    def vm(*shape):
        return pltpu.VMEM(shape, BF)

    return pl.pallas_call(
        layer_kernel,
        out_shape=(
            sds((128, 2048)), sds((128, 2048)), sds((64, 512)), sds((64, 512)),
            sds((32, 64, 512)), sds((32, 64, 512)),
        ),
        in_specs=[SM, VM, VM, VM, VM, VM, ANY, ANY],
        out_specs=(VM, VM, VM, VM, ANY, ANY),
        scratch_shapes=[
            vm(32, 16, 512), vm(32, 512), vm(4, 64, 16, 512), vm(4, 2, 32, 512),
            vm(2048, 512), vm(512, 2048), vm(2048, 512), vm(512, 2048),
            vm(1024, 512), vm(256, 2048), vm(1024, 512), vm(256, 2048),
            vm(2, 128, 512), vm(2, 32, 2048), vm(2, 256, 512), vm(2, 64, 2048),
            vm(4, 256, 512), vm(4, 64, 2048),
            vm(32, 16, 128), vm(4, 64, 16, 128), vm(2, 512, 512), vm(2, 512, 512), vm(2, 512, 512),
            vm(512, 512), vm(512, 512),
            vm(8, 512, 512), vm(8, 128, 512),
            vm(2048, 512), vm(2048, 512), vm(4, 64, 16, 512), vm(4, 2, 32, 512),
            vm(32, 1024), vm(32, 32, 128),
            vm(2, 4, 8, 16, 512), vm(2, 8, 8, 16, 512), vm(64, 16, 512), vm(64, 16, 512),
            vm(3, 2, 32, 512), vm(2, 32, 512), vm(2, 32, 512), vm(4, 4, 2, 32, 1024), vm(32, 32, 128),
            DMA((2,)), DMA, DMA((8,)), DMA, DMA((2, 8)), DMA((8,)), DMA, DMA((2,)), DMA, DMA,
            DMA((2,)), DMA((2,)), DMA((2,)),
            DMA((2, 6)), DMA((2, 2)), DMA((2, 2)), DMA((2, 2)),
            DMA((2, 2)), DMA((2, 2)),
            DMA((2, 6)), DMA((2, 2, 2)), DMA((2, 2)), DMA((2, 4)), DMA((2, 4)),
            DMA((2,)), DMA((2,)), DMA, DMA, DMA, DMA((2, 4)), DMA, DMA((2, 4)), DMA, DMA((2, 4)), DMA, DMA,
            DMA, DMA((3,)), DMA, DMA((2,)), DMA, DMA((4,)), DMA, DMA((3,)), DMA, DMA,
            DMA, DMA, DMA, DMA((2,)), DMA((2,)), DMA, DMA((4,)), DMA, DMA((2,)),
        ],
        compiler_params=pltpu.CompilerParams(
            collective_id=1, has_side_effects=True, vmem_limit_bytes=LIMIT
        ),
        name="layer",
    )(hot_mask, tokens, cotangent, gate_t, ids_t, slots_t, up, down)


def on_device(tokens, cotangent, gate_probs, expert_ids, route_slots, hot_mask, w_up, w_down):
    layer_out, grad_tokens, hup, hdn, ogu, ogd = layer(
        hot_mask, tokens, cotangent, gate_probs.T, expert_ids.T, route_slots.T, w_up[0], w_down[0]
    )
    is_hot = (hot_mask > 0)[:, None, None]
    grad_up = jnp.where(is_hot, hup[None], ogu)
    grad_down = jnp.where(is_hot, hdn[None], ogd)
    return (layer_out, grad_tokens, grad_up, grad_down)


def solution(mesh):
    placed = (
        P(("dp", "expert"), None),
        P(("dp", "expert"), None),
        P(("dp", "expert"), None),
        P(("dp", "expert"), None),
        P(("dp", "expert"), None),
        P(),
        P("expert", None, "dp"),
        P("expert", "dp", None),
    )
    return jax.shard_map(
        on_device,
        mesh=mesh,
        in_specs=placed,
        out_specs=(
            P(("dp", "expert"), None),
            P(("dp", "expert"), None),
            P(None, "expert", "dp"),
            P(None, "expert", "dp"),
        ),
        check_vma=False,
    )
```

```python
import functools

import jax
import jax.numpy as jnp
from jax import lax
from jax.experimental import pallas as pl
from jax.experimental.pallas import tpu as pltpu
from jax.sharding import PartitionSpec as P

CAP = 2
HCAP = 4
MESH = pl.DeviceIdType.MESH
BF = jnp.bfloat16
F32 = jnp.float32
ANY = pl.BlockSpec(memory_space=pl.ANY)
VM = pl.BlockSpec(memory_space=pltpu.VMEM)
SM = pl.BlockSpec(memory_space=pltpu.SMEM)
DMA = pltpu.SemaphoreType.DMA
Z_OFFSETS = (0, 1, 7, 2, 6, 3, 5, 4)
LIMIT = 60 * 1024 * 1024


def sds(shape, dtype=BF):
    return jax.ShapeDtypeStruct(shape, dtype)


def iota(shape, dim):
    return lax.broadcasted_iota(jnp.int32, shape, dim)


def dot(a, b):
    return jnp.dot(a, b, preferred_element_type=F32)


def dot_nt(a, b):
    return lax.dot_general(a, b, (((1,), (1,)), ((), ())), preferred_element_type=F32)


def dot_tn(a, b):
    return lax.dot_general(a, b, (((0,), (0,)), ((), ())), preferred_element_type=F32)


def ones_where(cond):
    return jnp.where(cond, 1.0, 0.0).astype(BF)


class Place:
    def __init__(self):
        self.dp = lax.axis_index("dp")
        self.e = lax.axis_index("expert")
        self.h = self.dp // 4
        self.y = self.dp % 4
        self.z = self.e // 8
        self.x = (self.e // 2) % 4
        self.c = self.e % 2
        self.me = self.h * 32 + self.e
        self.group = self.me // 8

    def at_y(self, y):
        return (self.h * 4 + y, self.e)

    def at_x(self, x):
        return (self.dp, self.z * 8 + x * 2 + self.c)

    def at_z(self, z):
        return (self.dp, z * 8 + self.x * 2 + self.c)

    def partner(self):
        return (self.dp, self.e + 1 - 2 * self.c)

    def at_peer(self, p):
        return ((p // 32) * 4 + self.y, p % 32)


def send(src, dst, ssem, rsem, to):
    copy = pltpu.make_async_remote_copy(
        src_ref=src, dst_ref=dst, send_sem=ssem, recv_sem=rsem, device_id=to, device_id_type=MESH
    )
    copy.start()


def local(src, dst, sem):
    pltpu.make_async_copy(src, dst, sem).start()


def wait(ref, sem):
    pltpu.make_async_copy(ref, ref, sem).wait()


def rows(start, size):
    return pl.ds(pl.multiple_of(start, 16), size)


def gelu_pair(preact):
    normal_cdf = 0.5 * (1.0 + lax.erf(preact * 0.7071067811865476))
    density = jnp.exp(-0.5 * preact * preact) * 0.3989422804014327
    return (preact * normal_cdf, normal_cdf + preact * density)


def order_matrix(src_count, slot_count):
    r = iota((256, 256), 0)
    k = iota((256, 256), 1)
    slot = r % slot_count
    src = (r // slot_count) % src_count
    q = (r // 32) % 4
    a = r // 128
    return ones_where(k == src * (8 * slot_count) + a * (4 * slot_count) + slot * 4 + q)


def to_column(row):
    wide = row.shape[1]
    same = iota((wide, wide), 0) == iota((wide, wide), 1)
    return jnp.sum(jnp.where(same, row, jnp.zeros_like(row)), axis=1, keepdims=True)


def places_of(ids, slot, hot):
    is_hot = ids == hot
    normal = jnp.where(jnp.logical_and(jnp.logical_not(is_hot), slot < CAP), ids * CAP + slot, -1)
    special = jnp.where(jnp.logical_and(is_hot, slot < HCAP), slot, -1)
    return normal, special


def pack_rows(hot, tokens, cot, gate_cols, ids, slots, disp, hrow):
    r = iota((512, 128), 0)
    code = (r // 16) * CAP + (r // 4) % 2
    is_grad = (r // 8) % 2
    quarter = r % 4
    hr = iota((32, 128), 0)
    hcode = (hr // 4) % 4
    h_is_grad = hr // 16
    hquarter = hr % 4
    sel, hsel = [], []
    for k in range(2):
        normal, special = places_of(ids[k : k + 1, :], slots[k : k + 1, :], hot)
        sel.append(code == normal)
        hsel.append(hcode == special)
    either = jnp.logical_or(sel[0], sel[1])
    heither = jnp.logical_or(hsel[0], hsel[1])
    out = jnp.zeros((512, 512), F32)
    hout = jnp.zeros((32, 512), F32)
    for q in range(4):
        cols = slice(q * 512, (q + 1) * 512)
        wide = cot[:, cols].astype(F32)
        parts = (
            (tokens[:, cols], either, heither, 0),
            ((gate_cols[0] * wide).astype(BF), sel[0], hsel[0], 1),
            ((gate_cols[1] * wide).astype(BF), sel[1], hsel[1], 1),
        )
        for data, s, hs, kind in parts:
            m = ones_where(jnp.logical_and(jnp.logical_and(s, quarter == q), is_grad == kind))
            out += dot(m, data)
            hm = ones_where(jnp.logical_and(jnp.logical_and(hs, hquarter == q), h_is_grad == kind))
            hout += dot(hm, data)
    disp[...] = out.astype(BF).reshape(32, 16, 512)
    hrow[...] = hout.astype(BF)


def pack_columns(hot, tokens, cot, gate_cols, ids, slots, edisp):
    r = iota((512, 128), 0)
    dest = r // 16
    z = dest // 8
    code = ((2 - z // 2) * 8 + dest % 8) * CAP + (r // 4) % 2
    is_grad = (r // 8) % 2
    piece = z * 4 + r % 4
    sel = [code == places_of(ids[k : k + 1, :], slots[k : k + 1, :], hot)[0] for k in range(2)]
    either = jnp.logical_or(sel[0], sel[1])
    masks = [
        jnp.logical_and(s, is_grad == kind) for s, kind in ((either, 0), (sel[0], 1), (sel[1], 1))
    ]
    for q in range(4):
        here = slice(q * 128, (q + 1) * 128)
        out = jnp.zeros((128, 128), F32)
        for p in range(4 * q, 4 * q + 4):
            cols = slice(p * 128, (p + 1) * 128)
            wide = cot[:, cols].astype(F32)
            data = (tokens[:, cols], (gate_cols[0] * wide).astype(BF), (gate_cols[1] * wide).astype(BF))
            for d, mask in zip(data, masks):
                out += dot(ones_where(jnp.logical_and(mask, piece == p)[here]), d)
        edisp[q * 8 : (q + 1) * 8] = out.astype(BF).reshape(8, 16, 128)


def make_picks(hot, id_cols, slot_cols, picks, hpicks):
    r = iota((128, 1024), 1)
    code = ((r // 16) % 32) * CAP + (r // 4) % 2
    is_back = (r // 8) % 2
    quarter = r % 4
    hr = iota((128, 64), 1)
    hcode = (hr // 4) % 4
    h_is_back = (hr // 16) % 2
    hquarter = hr % 4
    sel, hsel = [], []
    for k in range(2):
        normal, special = places_of(id_cols[k], slot_cols[k], hot)
        sel.append(code == normal)
        hsel.append(hcode == special)
    sel.append(jnp.logical_or(sel[0], sel[1]))
    hsel.append(jnp.logical_or(hsel[0], hsel[1]))
    for q in range(4):
        for k, kind in ((0, 0), (1, 0), (2, 1)):
            picks[q * 3 + k] = ones_where(
                jnp.logical_and(jnp.logical_and(sel[k], quarter == q), is_back == kind)
            )
            hpicks[q * 3 + k] = ones_where(
                jnp.logical_and(jnp.logical_and(hsel[k], hquarter == q), h_is_back == kind)
            )


def combine_rows(picks, hpicks, rbuf, rhot, gate_cols, out_ref, back_ref):
    data = rbuf[...].reshape(1024, 512)
    hdata = rhot[...].reshape(64, 512)
    for q in range(4):
        cols = slice(q * 512, (q + 1) * 512)
        got = [dot(picks[q * 3 + k], data) + dot(hpicks[q * 3 + k], hdata) for k in range(3)]
        out_ref[:, cols] = (gate_cols[0] * got[0] + gate_cols[1] * got[1]).astype(BF)
        back_ref[:, cols] = got[2].astype(BF)


def layer_kernel(
    mask_ref, tokens, cot, gate_ref, ids_ref, slots_ref, up, down,
    out_ref, back_ref, hup_ref, hdn_ref, ogu, ogd,
    disp, hrow, buf, hbuf, upv, dnv, uph, dnh,
    p_up, p_dn, o_up, o_dn, m_up, m_dn, r_up, r_dn, t_up, t_dn,
    edisp, ebuf, xe, pa, epa, egu, egd, picks, hpicks,
    xs, ys, gu, gd, parts, hparts, apack, wsend,
    m, r, ret, rbuf, hr, hret, rhot, apool, wrecv,
    load_s, disp_s, disp_r, y_s, y_r, y_f, h_s, h_r, hy_s, hy_r,
    s1_s, s1_r, s1_l, s2_s, s2_m, s2_raw, s2_acc, s3_s, s3_r, s5_s, s5_r, s5_f, s6_s, s6_r,
    g_s, g_r, w_s, w_r, m_s, m_r, raw_s, raw_r, acc_s, acc_r, ret_s, ret_r,
    hp_s, hp_r, hret_s, hret_r, az_s, az_r, ax_s, ax_r, ac_s, ac_r,
    ed_s, ed_r, ey_s, ey_r, ey_f, em_s, em_r, ef_s, eg_s,
):
    at = Place()
    y, x, z, c = at.y, at.x, at.z, at.c
    yr, yl, yo = (y + 1) % 4, (y + 3) % 4, (y + 2) % 4
    xr, xl, xo = (x + 1) % 4, (x + 3) % 4, (x + 2) % 4

    barrier = pltpu.get_barrier_semaphore()

    def greet(k, _):
        pl.semaphore_signal(barrier, inc=1, device_id=at.at_peer((at.me + k) % 64), device_id_type=MESH)
        return 0

    lax.fori_loop(1, 64, greet, 0)
    for k in range(1, 4):
        pl.semaphore_signal(barrier, inc=1, device_id=at.at_y((y + k) % 4), device_id_type=MESH)

    arrays = ((up, o_up, p_up, 1024), (down, o_dn, p_dn, 256))
    for i, (w, own, _, n) in enumerate(arrays):
        local(w.at[rows(c * n, n)], own, s1_l.at[i])
    local(up, upv, load_s.at[0])
    local(down, dnv, load_s.at[1])

    hot = mask_ref[0] * 0
    for k in range(1, 32):
        hot += mask_ref[k] * k
    f_own = jnp.where(hot == at.e, 1.0, 0.0)
    f_other = jnp.where(hot == at.e + 1 - 2 * c, 1.0, 0.0)
    gate_cols = [to_column(gate_ref[k : k + 1, :]) for k in range(2)]
    pack_rows(hot, tokens, cot, gate_cols, ids_ref, slots_ref, disp, hrow)

    pl.semaphore_wait(barrier, 66)

    for i, (w, _, other, n) in enumerate(arrays):
        send(w.at[rows((1 - c) * n, n)], other, s1_s.at[i], s1_r.at[i], at.partner())

    local(disp.at[at.e], buf.at[y, at.me], disp_r.at[at.group])
    groups = [(at.group + off) % 8 for off in Z_OFFSETS]
    for i, off in enumerate(Z_OFFSETS):

        def dispatch(k, _, g=groups[i]):
            p = g * 8 + (at.me + k) % 8
            send(disp.at[p % 32], buf.at[y, at.me], disp_s, disp_r.at[at.group], at.at_peer(p))
            return 0

        lax.fori_loop(1 if i == 0 else 0, 8, dispatch, 0)
    local(hrow, hbuf.at[y, at.h], h_r.at[0])
    send(hrow, hbuf.at[y, at.h], h_s, h_r.at[1], at.at_peer((at.me + 32) % 64))

    for i, (w, own, other, n) in enumerate(arrays):
        wait(own, s1_l.at[i])
        wait(other, s1_r.at[i])
    for own, other, n in ((o_up, p_up, 1024), (o_dn, p_dn, 256)):

        def choose(k, _, own=own, other=other, n=n):
            s = rows(k * (n // 16), n // 16)
            own[s] = (own[s].astype(F32) * f_own + other[s].astype(F32) * f_other).astype(BF)
            return 0

        lax.fori_loop(0, 16, choose, 0)

    ring = ((o_up, m_up, r_up, t_up, 128), (o_dn, m_dn, r_dn, t_dn, 32))
    full = ((uph, t_up, r_up, 64), (dnh, t_dn, r_dn, 16))

    def hot_begin(i):
        o, mm, rr, t, n = ring[i]
        send(o.at[rows(xo * 2 * n, n)], mm.at[0], s2_s.at[i, 0], s2_m.at[i, 0], at.at_x(xr))
        send(o.at[rows(xo * 2 * n + n, n)], mm.at[1], s2_s.at[i, 1], s2_m.at[i, 1], at.at_x(xl))
        send(o.at[rows(xr * 2 * n + n, n)], rr.at[0, pl.ds(n, n)], s2_s.at[i, 2], s2_raw.at[i, 0], at.at_x(xr))
        send(o.at[rows(xl * 2 * n, n)], rr.at[1, pl.ds(0, n)], s2_s.at[i, 3], s2_raw.at[i, 1], at.at_x(xl))

    def hot_ring(i):
        o, mm, rr, t, n = ring[i]
        wait(mm.at[0], s2_m.at[i, 0])
        mm[0] = mm[0] + o[rows(xr * 2 * n, n)]
        send(mm.at[0], rr.at[0, pl.ds(0, n)], s2_s.at[i, 4], s2_acc.at[i, 0], at.at_x(xr))
        wait(mm.at[1], s2_m.at[i, 1])
        mm[1] = mm[1] + o[rows(xl * 2 * n + n, n)]
        send(mm.at[1], rr.at[1, pl.ds(n, n)], s2_s.at[i, 5], s2_acc.at[i, 1], at.at_x(xl))

    def hot_line(i):
        o, mm, rr, t, n = ring[i]
        for side, raw, acc in ((0, pl.ds(n, n), pl.ds(0, n)), (1, pl.ds(0, n), pl.ds(n, n))):
            wait(rr.at[side, raw], s2_raw.at[i, side])
            wait(rr.at[side, acc], s2_acc.at[i, side])
        rr[0] = rr[0] + rr[1] + o[rows(x * 2 * n, 2 * n)]

        @pl.when(z == 0)
        def _():
            send(rr.at[0], t.at[0], s3_s.at[i, 0], s3_r.at[i, 0], at.at_z(1))

        @pl.when(z == 3)
        def _():
            send(rr.at[0], t.at[1], s3_s.at[i, 1], s3_r.at[i, 1], at.at_z(2))

    def hot_up(i):
        o, mm, rr, t, n = ring[i]

        @pl.when(z > 0)
        def _():
            wait(t.at[0], s3_r.at[i, 0])

            @pl.when(z < 3)
            def _():
                t[2] = t[0] + rr[0]
                send(t.at[2], t.at[0], s3_s.at[i, 0], s3_r.at[i, 0], at.at_z(z + 1))

    def hot_down(i):
        o, mm, rr, t, n = ring[i]

        @pl.when(z < 3)
        def _():
            wait(t.at[1], s3_r.at[i, 1])

            @pl.when(z > 0)
            def _():
                t[3] = t[1] + rr[0]
                send(t.at[3], t.at[1], s3_s.at[i, 1], s3_r.at[i, 1], at.at_z(z - 1))

    def hot_near():
        @pl.when(z < 2)
        def _():
            hot_up(0)
            hot_up(1)

        @pl.when(z >= 2)
        def _():
            hot_down(0)
            hot_down(1)

    def hot_far():
        @pl.when(z < 2)
        def _():
            hot_down(0)
            hot_down(1)

        @pl.when(z >= 2)
        def _():
            hot_up(0)
            hot_up(1)

    def half_of(dst, w):
        return lambda xx, b: dst.at[rows(c * 16 * w + xx * 4 * w + b * 2 * w, 2 * w)]

    def quarter_of(dst, w, xx):
        return dst.at[rows(c * 16 * w + xx * 4 * w, 4 * w)]

    def hot_around(i):
        dst, t, rr, w = full[i]
        mine = rows(c * 16 * w + x * 4 * w, 4 * w)

        @pl.when(z == 0)
        def _():
            dst[mine] = rr[0] + t[1]

        @pl.when(z == 3)
        def _():
            dst[mine] = rr[0] + t[0]

        @pl.when(jnp.logical_and(z > 0, z < 3))
        def _():
            dst[mine] = rr[0] + t[0] + t[1]

        half = half_of(dst, w)
        for b in range(2):
            send(half(x, b), half(x, b), s5_s.at[i, b], s5_r.at[i, 0, b], at.at_x(xr))
            send(half(x, 1 - b), half(x, 1 - b), s5_s.at[i, 2 + b], s5_r.at[i, 1, 1 - b], at.at_x(xl))
        send(quarter_of(dst, w, x), quarter_of(dst, w, x), s6_s.at[i, 0], s6_r.at[i, 0], at.partner())

    def hot_onward(i):
        dst, t, rr, w = full[i]
        half = half_of(dst, w)
        wait(half(xl, 0), s5_r.at[i, 0, 0])
        send(half(xl, 0), half(xl, 0), s5_s.at[i, 4], s5_f.at[i, 0], at.at_x(xr))
        wait(half(xr, 1), s5_r.at[i, 1, 1])
        send(half(xr, 1), half(xr, 1), s5_s.at[i, 5], s5_f.at[i, 1], at.at_x(xl))

    def hot_partner(i):
        dst, t, rr, w = full[i]
        half = half_of(dst, w)
        wait(half(xl, 1), s5_r.at[i, 0, 1])
        wait(half(xr, 0), s5_r.at[i, 1, 0])
        for k, xx in ((1, xl), (2, xr)):
            send(quarter_of(dst, w, xx), quarter_of(dst, w, xx), s6_s.at[i, k], s6_r.at[i, k], at.partner())

    def hot_last(i):
        dst, t, rr, w = full[i]
        half = half_of(dst, w)
        wait(half(xo, 0), s5_f.at[i, 0])
        wait(half(xo, 1), s5_f.at[i, 1])
        send(quarter_of(dst, w, xo), quarter_of(dst, w, xo), s6_s.at[i, 3], s6_r.at[i, 3], at.partner())

    def hot_arrived():
        for i, (dst, t, rr, w) in enumerate(full):
            for k in range(4):
                wait(dst.at[pl.ds(0, 4 * w)], s6_r.at[i, k])

    for i in range(2):
        hot_begin(i)

    def slab(of_y, g):
        return buf.at[of_y, pl.ds(g * 8, 8)]

    def pass_on(i):
        g = groups[i]
        wait(slab(y, g), disp_r.at[g])
        send(slab(y, g), slab(y, g), y_s, y_r.at[0, i], at.at_y(yr))
        send(slab(y, g), slab(y, g), y_s, y_r.at[1, i], at.at_y(yl))

    def forward(i):
        g = groups[i]
        wait(slab(yl, g), y_r.at[0, i])
        if i % 2 == 0:
            send(slab(yl, g), slab(yl, g), y_s, y_f.at[i], at.at_y(yr))
        wait(slab(yr, g), y_r.at[1, i])
        if i % 2 == 1:
            send(slab(yr, g), slab(yr, g), y_s, y_f.at[i], at.at_y(yl))

    order = order_matrix(16, 2)

    def hidden(s):
        def sort_rows(b, _):
            data = buf[s, pl.ds(b * 16, 16)].reshape(256, 512)
            block = dot(order, data).astype(BF)
            for k in range(8):
                xs[k, rows(s * 128 + b * 32, 32)] = block[k * 32 : (k + 1) * 32]
            return 0

        lax.fori_loop(0, 4, sort_rows, 0)
        at_s = rows(s * 128, 128)
        preact = dot(xs[0, at_s], upv[0:512])
        dact = dot_nt(xs[4, at_s], dnv[:, 0:512])
        for q in range(1, 4):
            preact += dot(xs[q, at_s], upv[q * 512 : (q + 1) * 512])
            dact += dot_nt(xs[4 + q, at_s], dnv[:, q * 512 : (q + 1) * 512])
        value, slope = gelu_pair(preact)
        pa[1, at_s] = value.astype(BF)
        pa[0, at_s] = (dact * slope).astype(BF)

    inner = jnp.logical_or(z == 1, z == 2)

    def share(i, s):
        at_s = rows(s * 128, 128)

        @pl.when(inner)
        def _():
            send(pa.at[:, at_s], epa.at[:, at_s], em_s, em_r.at[i], at.at_z(3 - z))

    def share_outward(i, s):
        at_s = rows(s * 128, 128)
        wait(epa.at[:, at_s], em_r.at[i])

        @pl.when(inner)
        def _():
            send(epa.at[:, at_s], epa.at[:, at_s], ef_s, em_r.at[i], at.at_z(3 * (z - 1)))

    for i in range(5):
        pass_on(i)
    hot_ring(0)
    hot_ring(1)
    for i in range(5, 8):
        pass_on(i)

    wait(hbuf.at[y, at.h], h_r.at[0])
    wait(hbuf.at[y, 1 - at.h], h_r.at[1])
    for k in range(1, 4):
        send(hbuf.at[y], hbuf.at[y], hy_s, hy_r, at.at_y((y + k) % 4))

    forward(0)
    forward(1)
    pack_columns(hot, tokens, cot, gate_cols, ids_ref, slots_ref, edisp)
    local(edisp.at[at.e], ebuf.at[y, at.me], ed_r)

    def dispatch_columns(k, _):
        p = (at.me + k) % 64
        send(edisp.at[p % 32], ebuf.at[y, at.me], ed_s, ed_r, at.at_peer(p))
        return 0

    lax.fori_loop(1, 64, dispatch_columns, 0)
    forward(2)
    forward(3)
    wait(upv, load_s.at[0])
    wait(dnv, load_s.at[1])
    hidden(y)
    share(0, y)
    hot_line(0)
    hot_line(1)
    for i in range(4, 8):
        forward(i)
    hot_near()
    hidden(yl)
    share(1, yl)
    wait(ebuf.at[y], ed_r)
    send(ebuf.at[y], ebuf.at[y], ey_s, ey_r.at[0], at.at_y(yr))
    send(ebuf.at[y], ebuf.at[y], ey_s, ey_r.at[1], at.at_y(yl))
    share_outward(0, y)
    hidden(yr)
    share(2, yr)
    hot_far()

    wait(hbuf.at[pl.ds(0, 3)], hy_r)
    horder = order_matrix(8, 4)
    hx = dot(horder, hbuf[...].reshape(256, 512)).astype(BF)
    hx = [hx[k * 32 : (k + 1) * 32] for k in range(8)]
    i0 = iota((128, 128), 0)
    j0 = iota((128, 128), 1)
    for odd in range(2):
        take_in = ones_where(jnp.logical_and(j0 < 64, i0 == j0 + 64 * odd))
        take_grad = ones_where(jnp.logical_and(j0 >= 64, i0 == j0 - 64 + 64 * odd))
        for b in range(16):
            q, o = b // 4, (b % 4) * 128
            block = dot(hx[q][:, o : o + 128], take_in) + dot(hx[4 + q][:, o : o + 128], take_grad)
            wsend[2 * b + odd] = block.astype(BF)
    local(wsend.at[at.e], wrecv.at[at.e], w_r)

    def widths(k, _):
        e = (at.e + k) % 32
        send(wsend.at[e], wrecv.at[at.e], w_s, w_r, (at.dp, e))
        return 0

    lax.fori_loop(1, 32, widths, 0)

    hot_around(0)
    hot_around(1)
    share_outward(1, yl)
    for i in range(8):
        wait(slab(yo, groups[i]), y_f.at[i])
    hidden(yo)
    share(3, yo)
    share_outward(2, yr)

    local_at = rows(at.e * 64, 64)

    def gradients(q):
        here = rows(q * 512, 512)
        gu[here] = dot_tn(xs[q], pa[0]).astype(BF)
        gd[here] = dot_tn(xs[4 + q], pa[1]).astype(BF)

    def give_gradients(k, _, q):
        e = q * 8 + (at.e + k) % 8
        to = (at.dp, e)
        send(gu.at[rows(e * 64, 64)], ogu.at[at.e], g_s.at[0], g_r.at[0], to)
        send(gd.at[rows(e * 64, 64)], ogd.at[at.e], g_s.at[1], g_r.at[1], to)
        return 0

    def partial(s):
        at_s = rows(s * 128, 128)
        for q in range(4):
            cols = slice(q * 512, (q + 1) * 512)
            ys[q] = dot(pa[1, at_s], dnv[:, cols]).astype(BF)
            ys[4 + q] = dot_nt(pa[0, at_s], upv[cols, :]).astype(BF)

        def unsort_rows(b, _):
            block = jnp.concatenate([ys[k, rows(b * 32, 32)] for k in range(8)], axis=0)
            parts[s, pl.ds(b * 16, 16)] = dot_tn(order, block).astype(BF).reshape(16, 16, 512)
            return 0

        lax.fori_loop(0, 4, unsort_rows, 0)

    def part(of_y, g):
        return parts.at[of_y, pl.ds(g * 8, 8)]

    def direct(k):
        q = (z + k) % 4
        crosses = (z // 2) != (q // 2)

        @pl.when(jnp.logical_not(jnp.logical_and(inner, crosses)))
        def _():
            gradients(q)
            lax.fori_loop(0, 8, functools.partial(give_gradients, q=q), 0)

    direct(2)
    direct(1)
    share_outward(3, yo)
    partial(yo)
    for i in range(4):
        send(part(yo, i), m.at[0, i], m_s, m_r.at[0, i], at.at_y(yr))
        send(part(yo, 4 + i), m.at[1, i], m_s, m_r.at[1, i], at.at_y(yl))
    hot_onward(0)
    hot_onward(1)
    wait(ebuf.at[yl], ey_r.at[0])
    send(ebuf.at[yl, pl.ds(0, 32)], ebuf.at[yl, pl.ds(0, 32)], ey_s, ey_f.at[0], at.at_y(yr))
    wait(ebuf.at[yr], ey_r.at[1])
    send(ebuf.at[yr, pl.ds(32, 32)], ebuf.at[yr, pl.ds(32, 32)], ey_s, ey_f.at[1], at.at_y(yl))
    direct(3)
    for s, to, first, side in ((yr, yr, 4, 0), (yl, yl, 0, 1)):
        partial(s)
        for i in range(4):
            send(part(s, first + i), r.at[side, first + i], raw_s, raw_r.at[side, i], at.at_y(to))
    gradients(z)
    local(gu.at[local_at], ogu.at[at.e], g_r.at[0])
    local(gd.at[local_at], ogd.at[at.e], g_r.at[1])
    lax.fori_loop(1, 8, functools.partial(give_gradients, q=z), 0)


    for i in range(4):
        wait(m.at[0, i], m_r.at[0, i])
        m[0, i] = (m[0, i].astype(F32) + parts[yr, pl.ds(i * 8, 8)].astype(F32)).astype(BF)
        send(m.at[0, i], r.at[0, i], acc_s, acc_r.at[0, i], at.at_y(yr))
        wait(m.at[1, i], m_r.at[1, i])
        m[1, i] = (m[1, i].astype(F32) + parts[yl, pl.ds(32 + i * 8, 8)].astype(F32)).astype(BF)
        send(m.at[1, i], r.at[1, 4 + i], acc_s, acc_r.at[1, i], at.at_y(yl))
    wait(ebuf.at[yo, pl.ds(0, 32)], ey_f.at[0])
    wait(ebuf.at[yo, pl.ds(32, 32)], ey_f.at[1])

    def sort_columns(b, _):
        s = b // 4
        data = ebuf[s, pl.ds((b % 4) * 16, 16)].reshape(256, 128)
        block = dot(order, data).astype(BF)
        for k in range(8):
            xe[k // 4, rows(b * 32, 32), (k % 4) * 128 : (k % 4 + 1) * 128] = block[k * 32 : (k + 1) * 32]
        return 0

    lax.fori_loop(0, 16, sort_columns, 0)
    egu[...] = dot_tn(xe[0], epa[0]).astype(BF)
    egd[...] = dot_tn(xe[1], epa[1]).astype(BF)
    other_expert = (2 - z // 2) * 8 + at.e % 8
    local(egu.at[rows((at.e % 8) * 64, 64)], ogu.at[other_expert], g_r.at[0])
    local(egd.at[rows((at.e % 8) * 64, 64)], ogd.at[other_expert], g_r.at[1])

    def give_other(k, _):
        j = (at.e + k) % 8
        to = (at.dp, z * 8 + j)
        send(egu.at[rows(j * 64, 64)], ogu.at[other_expert], eg_s.at[0], g_r.at[0], to)
        send(egd.at[rows(j * 64, 64)], ogd.at[other_expert], eg_s.at[1], g_r.at[1], to)
        return 0

    lax.fori_loop(1, 8, give_other, 0)
    partial(y)

    hot_partner(0)
    hot_partner(1)
    hot_last(0)
    hot_last(1)

    hot_arrived()

    preact = dot(hx[0], uph[0:512])
    dact = dot_nt(hx[4], dnh[:, 0:512])
    for q in range(1, 4):
        preact += dot(hx[q], uph[q * 512 : (q + 1) * 512])
        dact += dot_nt(hx[4 + q], dnh[:, q * 512 : (q + 1) * 512])
    value, slope = gelu_pair(preact)
    hact = value.astype(BF)
    hpre = (dact * slope).astype(BF)
    apack[:, 0:512] = hpre
    apack[:, 512:1024] = hact
    local(apack, apool.at[z, x, c], az_r.at[3])
    for k in range(1, 4):
        send(apack, apool.at[z, x, c], az_s, az_r.at[k - 1], at.at_z((z + k) % 4))
    outs = [dot(hact, dnh[:, q * 512 : (q + 1) * 512]).astype(BF) for q in range(4)]
    backs = [dot_nt(hpre, uph[q * 512 : (q + 1) * 512, :]).astype(BF) for q in range(4)]
    hout = dot_tn(horder, jnp.concatenate(outs + backs, axis=0)).astype(BF)
    hparts[...] = hout.reshape(4, 2, 32, 512)
    for k in range(1, 4):
        yy = (y + k) % 4
        send(hparts.at[yy], hr.at[k - 1], hp_s, hp_r.at[k - 1], at.at_y(yy))

    for i in range(8):
        side_raw, side_acc = (1, 0) if i < 4 else (0, 1)
        wait(r.at[side_raw, i], raw_r.at[side_raw, i % 4])
        wait(r.at[side_acc, i], acc_r.at[side_acc, i % 4])
        ret[pl.ds(i * 8, 8)] = (
            parts[y, pl.ds(i * 8, 8)].astype(F32) + r[0, i].astype(F32) + r[1, i].astype(F32)
        ).astype(BF)

        def give_back(j, _, i=i):
            p = i * 8 + j

            @pl.when(p != at.me)
            def _():
                send(ret.at[p], rbuf.at[at.me], ret_s, ret_r, at.at_peer(p))

            @pl.when(p == at.me)
            def _():
                local(ret.at[p], rbuf.at[p], ret_r)

            return 0

        lax.fori_loop(0, 8, give_back, 0)

    for k in range(4):
        wait(apack, az_r.at[k])
    for k in range(1, 4):
        send(apool.at[:, x, c], apool.at[:, x, c], ax_s, ax_r.at[k - 1], at.at_x((x + k) % 4))
    for k in range(3):
        wait(hr.at[k], hp_r.at[k])
    hret[...] = (
        hparts[y].astype(F32) + hr[0].astype(F32) + hr[1].astype(F32) + hr[2].astype(F32)
    ).astype(BF)
    local(hret.at[at.h], rhot.at[at.h], hret_r.at[0])
    send(hret.at[1 - at.h], rhot.at[at.h], hret_s, hret_r.at[1], at.at_peer((at.me + 32) % 64))
    id_cols = [to_column(ids_ref[k : k + 1, :]) for k in range(2)]
    slot_cols = [to_column(slots_ref[k : k + 1, :]) for k in range(2)]
    make_picks(hot, id_cols, slot_cols, picks, hpicks)
    for k in range(3):
        wait(apool.at[:, 0, 0], ax_r.at[k])
    send(apool.at[:, :, c], apool.at[:, :, c], ac_s, ac_r, at.partner())

    wait(wrecv, w_r)
    wait(apool.at[:, :, 0], ac_r)
    wide = wrecv[...].reshape(1024, 128)
    pool = apool[...].reshape(1024, 1024)
    hup_ref[...] = dot_tn(wide, pool[:, 0:512])[0:64].astype(BF)
    hdn_ref[...] = dot_tn(wide, pool[:, 512:1024])[64:128].astype(BF)

    wait(rbuf, ret_r)
    wait(rhot.at[0], hret_r.at[0])
    wait(rhot.at[0], hret_r.at[1])
    combine_rows(picks, hpicks, rbuf, rhot, gate_cols, out_ref, back_ref)

    wait(ogu, g_r.at[0])
    wait(ogd, g_r.at[1])

    for i, (w, own, other, n) in enumerate(arrays):
        wait(own, s1_s.at[i])
    wait(buf.at[0, pl.ds(0, 63)], disp_s)
    wait(buf.at[pl.ds(0, 3)], y_s)
    wait(hbuf.at[pl.ds(0, 3)], hy_s)
    wait(hbuf.at[0, 0], h_s)
    for i, (o, mm, rr, t, n) in enumerate(ring):
        for k in range(6):
            wait(mm.at[0], s2_s.at[i, k])

        @pl.when(z < 3)
        def _(i=i, t=t):
            wait(t.at[0], s3_s.at[i, 0])

        @pl.when(z > 0)
        def _(i=i, t=t):
            wait(t.at[0], s3_s.at[i, 1])

    for i, (dst, t, rr, w) in enumerate(full):
        for k in range(6):
            wait(dst.at[pl.ds(0, 2 * w)], s5_s.at[i, k])
        for k in range(4):
            wait(dst.at[pl.ds(0, 4 * w)], s6_s.at[i, k])
    @pl.when(jnp.logical_not(inner))
    def _():
        wait(gu.at[pl.ds(0, 31 * 64)], g_s.at[0])
        wait(gd.at[pl.ds(0, 31 * 64)], g_s.at[1])

    @pl.when(inner)
    def _():
        wait(gu.at[pl.ds(0, 15 * 64)], g_s.at[0])
        wait(gd.at[pl.ds(0, 15 * 64)], g_s.at[1])
        wait(epa, em_s)
        wait(epa, ef_s)

    wait(egu.at[pl.ds(0, 7 * 64)], eg_s.at[0])
    wait(egd.at[pl.ds(0, 7 * 64)], eg_s.at[1])
    wait(ebuf.at[0, pl.ds(0, 63)], ed_s)
    wait(ebuf.at[pl.ds(0, 3)], ey_s)
    wait(wsend.at[pl.ds(0, 31)], w_s)
    wait(m, m_s)
    wait(m, raw_s)
    wait(m, acc_s)
    wait(ret.at[pl.ds(0, 63)], ret_s)
    wait(hr, hp_s)
    wait(hret.at[0], hret_s)
    wait(apool.at[0, 0:3, 0], az_s)
    wait(apool.at[:, 0:3, 0], ax_s)
    wait(apool.at[:, :, 0], ac_s)


def layer(hot_mask, tokens, cotangent, gate_t, ids_t, slots_t, up, down):
    def vm(*shape):
        return pltpu.VMEM(shape, BF)

    return pl.pallas_call(
        layer_kernel,
        out_shape=(
            sds((128, 2048)), sds((128, 2048)), sds((64, 512)), sds((64, 512)),
            sds((32, 64, 512)), sds((32, 64, 512)),
        ),
        in_specs=[SM, VM, VM, VM, VM, VM, ANY, ANY],
        out_specs=(VM, VM, VM, VM, ANY, ANY),
        scratch_shapes=[
            vm(32, 16, 512), vm(32, 512), vm(4, 64, 16, 512), vm(4, 2, 32, 512),
            vm(2048, 512), vm(512, 2048), vm(2048, 512), vm(512, 2048),
            vm(1024, 512), vm(256, 2048), vm(1024, 512), vm(256, 2048),
            vm(2, 128, 512), vm(2, 32, 2048), vm(2, 256, 512), vm(2, 64, 2048),
            vm(4, 256, 512), vm(4, 64, 2048),
            vm(32, 16, 128), vm(4, 64, 16, 128), vm(2, 512, 512), vm(2, 512, 512), vm(2, 512, 512),
            vm(512, 512), vm(512, 512), vm(12, 128, 1024), vm(12, 128, 64),
            vm(8, 512, 512), vm(8, 128, 512),
            vm(2048, 512), vm(2048, 512), vm(4, 64, 16, 512), vm(4, 2, 32, 512),
            vm(32, 1024), vm(32, 32, 128),
            vm(2, 4, 8, 16, 512), vm(2, 8, 8, 16, 512), vm(64, 16, 512), vm(64, 16, 512),
            vm(3, 2, 32, 512), vm(2, 32, 512), vm(2, 32, 512), vm(4, 4, 2, 32, 1024), vm(32, 32, 128),
            DMA((2,)), DMA, DMA((8,)), DMA, DMA((2, 8)), DMA((8,)), DMA, DMA((2,)), DMA, DMA,
            DMA((2,)), DMA((2,)), DMA((2,)),
            DMA((2, 6)), DMA((2, 2)), DMA((2, 2)), DMA((2, 2)),
            DMA((2, 2)), DMA((2, 2)),
            DMA((2, 6)), DMA((2, 2, 2)), DMA((2, 2)), DMA((2, 4)), DMA((2, 4)),
            DMA((2,)), DMA((2,)), DMA, DMA, DMA, DMA((2, 4)), DMA, DMA((2, 4)), DMA, DMA((2, 4)), DMA, DMA,
            DMA, DMA((3,)), DMA, DMA((2,)), DMA, DMA((4,)), DMA, DMA((3,)), DMA, DMA,
            DMA, DMA, DMA, DMA((2,)), DMA((2,)), DMA, DMA((4,)), DMA, DMA((2,)),
        ],
        compiler_params=pltpu.CompilerParams(
            collective_id=1, has_side_effects=True, vmem_limit_bytes=LIMIT
        ),
        name="layer",
    )(hot_mask, tokens, cotangent, gate_t, ids_t, slots_t, up, down)


def on_device(tokens, cotangent, gate_probs, expert_ids, route_slots, hot_mask, w_up, w_down):
    layer_out, grad_tokens, hup, hdn, ogu, ogd = layer(
        hot_mask, tokens, cotangent, gate_probs.T, expert_ids.T, route_slots.T, w_up[0], w_down[0]
    )
    is_hot = (hot_mask > 0)[:, None, None]
    grad_up = jnp.where(is_hot, hup[None], ogu)
    grad_down = jnp.where(is_hot, hdn[None], ogd)
    return (layer_out, grad_tokens, grad_up, grad_down)


def solution(mesh):
    placed = (
        P(("dp", "expert"), None),
        P(("dp", "expert"), None),
        P(("dp", "expert"), None),
        P(("dp", "expert"), None),
        P(("dp", "expert"), None),
        P(),
        P("expert", None, "dp"),
        P("expert", "dp", None),
    )
    return jax.shard_map(
        on_device,
        mesh=mesh,
        in_specs=placed,
        out_specs=(
            P(("dp", "expert"), None),
            P(("dp", "expert"), None),
            P(None, "expert", "dp"),
            P(None, "expert", "dp"),
        ),
        check_vma=False,
    )
```
